32 devices in a mesh: dp: 4 (over z), ctx: 8 (over y, x, core).
Axes of the slice: x: 2, y: 2, z: 4, core: 2. Of those that a mesh axis runs over, the one named last changes fastest.
Arguments:
- query_rows: bfloat16 [4, 1024, 2048], P('dp', 'ctx'), may hold values from -72 to 72
- key_rows: bfloat16 [4, 1024, 512], P('dp', 'ctx'), may hold values from -4 to 4
- value_rows: bfloat16 [4, 1024, 512], P('dp', 'ctx'), may hold values from -6 to 6
- grad_rows: bfloat16 [4, 1024, 2048], P('dp', 'ctx'), may hold values from -6 to 6
- bucket_rank: int32 [4, 1024], P('dp', 'ctx'), may hold values from 0 to 255, as said below
- sample_rows: int32 [4, 8], P('dp', 'ctx'), may hold values from 0 to 127, as said below
- sample_count: int32 [4, 8], P('dp', 'ctx'), may hold values from 1 to 3
- sink_logit: float32 [16], replicated, may hold values from 3 to 6
Outputs:
- query_grad: bfloat16 [4, 1024, 2048], P('dp', 'ctx')
- key_grad: bfloat16 [4, 1024, 512], P('dp', 'ctx')
- value_grad: bfloat16 [4, 1024, 512], P('dp', 'ctx')
- sink_grad: float32 [16], replicated
The draws below stay inside these ranges and needn't reach their ends.
Inputs may be any that keep to these rules, and one draw needn't show every extreme that they name: `bucket_rank`: for every sequence and every m, the values over the 256 tokens held by ctx indices 2m and 2m+1 are a permutation of 0 to 255. `sample_rows`: slot c names a row of the 128 tokens held by ctx index c, counted from that block's first token; the slots of one block name distinct rows.
All inputs are finite; a program needn't handle non-finite values.
Results may differ from the reference program's by a relative error of at most 0.0075.
Values may be sent and summed in bfloat16 or wider, within the bound.
No kernel may reach another device: no remote copies, remote signals or barrier semaphores. Data moves between devices by JAX's collectives and lax.ppermute only.
A program may use at most 64 MiB of HBM per device.

```python
from functools import partial
import jax
import jax.numpy as jnp
from jax import lax

HEADS = 16
KV_HEADS = 4
HDIM = 128
BUCKET = 128
TOK_DEV = 128
SAMP_DEV = 1
SEQS = 4
TOKENS = 1024
SAMPLES = 8


def query_key_pair(key):
    base = jax.random.fold_in(key, 4242)
    key_stream, query_stream = jax.random.split(base, 2)
    key_values = jax.random.truncated_normal(key_stream, -4.0, 4.0, (SEQS, TOKENS, KV_HEADS * HDIM), jnp.float32)
    query_values = jax.random.truncated_normal(query_stream, -4.0, 4.0, (SEQS, TOKENS, HEADS * HDIM), jnp.float32)
    return (query_values, key_values)


def draw_query_rows(key, part):
    return query_key_pair(key)[0].astype(jnp.bfloat16)


def draw_key_rows(key, part):
    return query_key_pair(key)[1].astype(jnp.bfloat16)


def draw_bucket_rank(key, part):
    pairs = TOKENS // (2 * TOK_DEV)
    streams = jax.random.split(jax.random.fold_in(key, 77), SEQS * pairs)
    orders = jax.vmap(lambda one_key: jax.random.permutation(one_key, 2 * TOK_DEV))(streams)
    return orders.reshape(SEQS, TOKENS).astype(jnp.int32)


def draw_sample_rows(key, part):
    blocks = TOKENS // TOK_DEV
    streams = jax.random.split(jax.random.fold_in(key, 91), SEQS * blocks)
    chosen = jax.vmap(lambda one_key: jax.random.permutation(one_key, TOK_DEV)[:SAMP_DEV])(streams)
    return chosen.reshape(SEQS, SAMPLES).astype(jnp.int32)


def with_ends(result, rng, smallest, top_value):
    spot = [jax.random.randint(jax.random.fold_in(rng, axis), (), 0, length) for axis, length in enumerate(result.shape)]
    widest = result.shape.index(max(result.shape))
    next_to = spot[:widest] + [(spot[widest] + 1) % result.shape[widest]] + spot[widest + 1:]
    return result.at[tuple(spot)].set(smallest).at[tuple(next_to)].set(top_value)


def block_levels(stream_key, shape, shards, least, top_value):
    def one(dim, blocks):
        steps = jax.random.uniform(jax.random.fold_in(jax.random.fold_in(stream_key, 6), dim), (blocks,), jnp.float32, least / len(shards), top_value / len(shards))
        return jnp.repeat(jnp.exp(steps), shape[dim] // blocks).reshape((-1,) + (1,) * (len(shape) - dim - 1))

    factor_of = one(*shards[0])
    for cut in shards[1:]:
        factor_of = factor_of * one(*cut)
    return factor_of


def normal_values(rng, dims, scale, bound, cuts=(), held_as=jnp.bfloat16):
    values = scale * jax.random.normal(rng, dims, jnp.float32)
    if cuts:
        values = values * block_levels(rng, dims, cuts, -0.22, 0.18)
    return jnp.clip(values, -bound, bound).astype(held_as)


def setup_inputs(seed: int = 0) -> dict:
    splits = jax.random.split(jax.random.key(seed), 9)
    return {
        "query_rows": draw_query_rows(jax.random.fold_in(splits[8], 71), 0),
        "key_rows": draw_key_rows(jax.random.fold_in(splits[8], 71), 0),
        "value_rows": normal_values(splits[2], (SEQS, TOKENS, KV_HEADS * HDIM), 1.0, 6.0, ((0, 4), (1, 8))),
        "grad_rows": normal_values(splits[3], (SEQS, TOKENS, HEADS * HDIM), 1.0, 6.0, ((0, 4), (1, 8))),
        "bucket_rank": draw_bucket_rank(jax.random.fold_in(splits[8], 71), 0),
        "sample_rows": draw_sample_rows(jax.random.fold_in(splits[8], 71), 0),
        "sample_count": with_ends(jax.random.randint(splits[6], (SEQS, SAMPLES), 1, 4), jax.random.fold_in(splits[6], 1), 1, 3).astype(jnp.int32),
        "sink_logit": jnp.clip(jax.random.uniform(splits[7], (HEADS,), jnp.float32, 3.0, 6.0), 3.0, 6.0),
    }


def one_sequence(items, sink_logit):
    query_seq, key_seq, value_seq, grad_seq, rank_seq, rows_seq, count_seq = items
    per_group = HEADS // KV_HEADS
    kv_width = KV_HEADS * HDIM
    score_scale = HDIM ** -0.5
    span = 2 * TOK_DEV
    blocks = TOKENS // span
    per_block = span // BUCKET
    token_index = jnp.arange(TOKENS, dtype=jnp.int32)
    position = (token_index // span) * span + rank_seq.astype(jnp.int32)
    ordered = jnp.zeros((TOKENS,), jnp.int32).at[position].set(token_index)
    slot_token = (jnp.arange(SAMPLES, dtype=jnp.int32) // SAMP_DEV) * TOK_DEV + rows_seq.astype(jnp.int32)
    slot_bucket = position[slot_token] // BUCKET
    log_weight = jnp.log(count_seq.astype(jnp.float32))
    sample_keys = key_seq[slot_token].astype(jnp.float32).reshape(SAMPLES, KV_HEADS, HDIM)
    sample_values = value_seq[slot_token].astype(jnp.float32).reshape(SAMPLES, KV_HEADS, HDIM)
    sink_row = sink_logit.reshape(KV_HEADS, per_group)
    sorted_query = query_seq[ordered].reshape(blocks, span, KV_HEADS, per_group, HDIM)
    sorted_keys = key_seq[ordered].reshape(blocks, span, KV_HEADS, HDIM)
    sorted_values = value_seq[ordered].reshape(blocks, span, KV_HEADS, HDIM)
    sorted_grads = grad_seq[ordered].reshape(blocks, span, KV_HEADS, per_group, HDIM)
    firsts = jnp.arange(blocks, dtype=jnp.int32) * span

    def block_pass(block_items):
        block_query, block_keys, block_values, block_grads, first_row = block_items
        query_flat = block_query.astype(jnp.float32)
        grad_flat = block_grads.astype(jnp.float32)
        query_bucket = (first_row + jnp.arange(span, dtype=jnp.int32)) // BUCKET
        query_split = query_flat.reshape(per_block, BUCKET, KV_HEADS, per_group, HDIM)
        grad_split = grad_flat.reshape(per_block, BUCKET, KV_HEADS, per_group, HDIM)
        key_split = block_keys.astype(jnp.float32).reshape(per_block, BUCKET, KV_HEADS, HDIM)
        value_split = block_values.astype(jnp.float32).reshape(per_block, BUCKET, KV_HEADS, HDIM)
        bucket_score = jnp.einsum("nikgd,njkd->nikgj", query_split, key_split) * score_scale
        bucket_score = bucket_score.reshape(span, KV_HEADS, per_group, BUCKET)
        sample_score = jnp.einsum("tkgd,ckd->tkgc", query_flat, sample_keys) * score_scale + log_weight
        excluded = query_bucket[:, None] == slot_bucket[None, :]
        sample_score = jnp.where(excluded[:, None, None, :], -jnp.inf, sample_score)
        row_max = jnp.maximum(jnp.maximum(jnp.max(bucket_score, -1), jnp.max(sample_score, -1)), sink_row)
        denominator = (jnp.exp(sink_row - row_max)
                       + jnp.sum(jnp.exp(bucket_score - row_max[..., None]), -1)
                       + jnp.sum(jnp.exp(sample_score - row_max[..., None]), -1))
        log_total = row_max + jnp.log(denominator)
        bucket_prob = jnp.exp(bucket_score - log_total[..., None])
        sample_prob = jnp.exp(sample_score - log_total[..., None])
        sink_prob = jnp.exp(sink_row - log_total)
        bucket_half = bucket_prob.astype(jnp.bfloat16).astype(jnp.float32)
        sample_half = sample_prob.astype(jnp.bfloat16).astype(jnp.float32)
        bucket_half_split = bucket_half.reshape(per_block, BUCKET, KV_HEADS, per_group, BUCKET)
        out_bucket = jnp.einsum("nikgj,njkd->nikgd", bucket_half_split, value_split).reshape(span, KV_HEADS, per_group, HDIM)
        out_sample = jnp.einsum("tkgc,ckd->tkgd", sample_half, sample_values)
        attended = (out_bucket + out_sample).astype(jnp.bfloat16).astype(jnp.float32)
        delta = jnp.sum(grad_flat * attended, -1)
        bucket_up = jnp.einsum("nikgd,njkd->nikgj", grad_split, value_split).reshape(span, KV_HEADS, per_group, BUCKET)
        sample_up = jnp.einsum("tkgd,ckd->tkgc", grad_flat, sample_values)
        bucket_ds = (bucket_prob * (bucket_up - delta[..., None])).astype(jnp.bfloat16).astype(jnp.float32)
        sample_ds = (sample_prob * (sample_up - delta[..., None])).astype(jnp.bfloat16).astype(jnp.float32)
        bucket_ds_split = bucket_ds.reshape(per_block, BUCKET, KV_HEADS, per_group, BUCKET)
        query_part = score_scale * (jnp.einsum("nikgj,njkd->nikgd", bucket_ds_split, key_split).reshape(span, KV_HEADS, per_group, HDIM)
                                    + jnp.einsum("tkgc,ckd->tkgd", sample_ds, sample_keys))
        key_part = score_scale * jnp.einsum("nikgj,nikgd->njkd", bucket_ds_split, query_split).reshape(span, KV_HEADS, HDIM)
        value_part = jnp.einsum("nikgj,nikgd->njkd", bucket_half_split, grad_split).reshape(span, KV_HEADS, HDIM)
        key_slot = score_scale * jnp.einsum("tkgc,tkgd->ckd", sample_ds, query_flat)
        value_slot = jnp.einsum("tkgc,tkgd->ckd", sample_half, grad_flat)
        sink_part = -jnp.sum(sink_prob * delta, 0)
        return query_part, key_part, value_part, key_slot, value_slot, sink_part

    query_part, key_part, value_part, key_slot, value_slot, sink_part = lax.map(
        block_pass, (sorted_query, sorted_keys, sorted_values, sorted_grads, firsts))
    query_grad = query_part.reshape(TOKENS, HEADS * HDIM)[position].astype(jnp.bfloat16)
    key_slot_sum = jnp.sum(key_slot, 0).reshape(SAMPLES, kv_width)
    value_slot_sum = jnp.sum(value_slot, 0).reshape(SAMPLES, kv_width)
    key_grad = (key_part.reshape(TOKENS, kv_width)[position]
                + jnp.zeros((TOKENS, kv_width), jnp.float32).at[slot_token].add(key_slot_sum)).astype(jnp.bfloat16)
    value_grad = (value_part.reshape(TOKENS, kv_width)[position]
                  + jnp.zeros((TOKENS, kv_width), jnp.float32).at[slot_token].add(value_slot_sum)).astype(jnp.bfloat16)
    return query_grad, key_grad, value_grad, jnp.sum(sink_part, 0).reshape(HEADS)


def reference(query_rows, key_rows, value_rows, grad_rows, bucket_rank, sample_rows, sample_count, sink_logit):
    results = lax.map(partial(one_sequence, sink_logit=sink_logit),
                      (query_rows, key_rows, value_rows, grad_rows, bucket_rank, sample_rows, sample_count))
    return results[0], results[1], results[2], jnp.sum(results[3], 0)
```

```python
import functools

import jax
import jax.numpy as jnp
from jax import lax
from jax.experimental import pallas as pl
from jax.experimental.pallas import tpu as pltpu
from jax.sharding import PartitionSpec as P

HEADS = 16
KV_HEADS = 4
HDIM = 128
BUCKET = 128
GROUP = HEADS // KV_HEADS
NEG = -1e30
PACK = 16
COUNT_ROW = 8
MARK_ROW = 9
TOKEN_MARK_ROW = 10

f32 = jnp.float32
bf16 = jnp.bfloat16
NT = (((1,), (1,)), ((), ()))
TN = (((0,), (0,)), ((), ()))
VMEM = pl.BlockSpec(memory_space=pltpu.VMEM)
SMEM = pl.BlockSpec(memory_space=pltpu.SMEM)


def moved(array, axis, apart):
    return lax.ppermute(array, axis, [(i, i ^ apart) for i in range(lax.axis_size(axis))])


def rounds(size, first):
    found, base = [], first
    while base < size:
        found.append([base] if base * 2 >= size else [base, 2 * base, 3 * base])
        base *= 2 if base * 2 >= size else 4
    return found


def iota(shape, dim):
    return lax.broadcasted_iota(jnp.int32, shape, dim)


def pack_kernel(row_ref, count_ref, keys_ref, values_ref, rank_ref, out_ref):
    length = keys_ref.shape[1]
    row = row_ref[0, 0]
    pick = (iota((PACK, length), 1) == row).astype(bf16)
    key = jnp.dot(pick, keys_ref[0], preferred_element_type=f32)
    value = jnp.dot(pick, values_ref[0], preferred_element_type=f32)
    marks = (rank_ref[...] >= BUCKET).astype(f32)
    lanes = iota((1, length), 1)
    mark = jnp.sum(jnp.where(lanes == row, marks, 0.0), axis=1, keepdims=True)
    rows = iota((PACK, HDIM), 0)
    tile = jnp.zeros((PACK, HDIM), f32)
    for j in range(KV_HEADS):
        tile = jnp.where(rows == j, key[:, j * HDIM : (j + 1) * HDIM], tile)
        tile = jnp.where(rows == KV_HEADS + j, value[:, j * HDIM : (j + 1) * HDIM], tile)
    tile = jnp.where(rows == COUNT_ROW, count_ref[0, 0].astype(f32), tile)
    tile = jnp.where(rows == MARK_ROW, mark, tile)
    tile = jnp.where(rows == TOKEN_MARK_ROW, marks, tile)
    out_ref[...] = tile.astype(bf16)


def main_kernel(
    slots, query_ref, grad_ref, keys_ref, values_ref, far_keys_ref, far_values_ref, packs_ref, sink_ref,
    dq_ref, own_ref, far_ref, keep_ref, send_ref, sinks_ref,
):
    length = query_ref.shape[1]
    padded = -(-slots // 16) * 16
    scale = HDIM**-0.5
    packs = packs_ref[...]

    def chosen(row):
        at = iota((padded, slots * PACK), 1)
        slot = iota((padded, slots * PACK), 0)
        return jnp.dot(
            (at == slot * PACK + row).astype(bf16), packs, preferred_element_type=f32
        )

    own_marks = packs[TOKEN_MARK_ROW : TOKEN_MARK_ROW + 1, :].astype(f32)
    far_marks = packs[PACK + TOKEN_MARK_ROW : PACK + TOKEN_MARK_ROW + 1, :].astype(f32)
    own_column = jnp.transpose(jnp.broadcast_to(own_marks, (length, length)))
    far_column = jnp.transpose(jnp.broadcast_to(far_marks, (length, length)))
    slot_at = iota((padded, length), 0)
    slot_bias = jnp.log(jnp.maximum(chosen(COUNT_ROW), 1.0))
    same = (slot_at < 2) & (chosen(MARK_ROW) == own_marks)
    slot_bias = jnp.where(same | (slot_at >= slots), NEG, slot_bias)
    bias = jnp.concatenate(
        [
            jnp.where(own_column == own_marks, 0.0, NEG),
            jnp.where(far_column == own_marks, 0.0, NEG),
            slot_bias,
        ],
        0,
    )
    bias = jnp.concatenate([bias] * GROUP, 1)
    sink_diag = iota((HEADS, HDIM), 0) == iota((HEADS, HDIM), 1)
    sinks = jnp.zeros((1, HDIM), f32)
    lane = iota((1, HDIM), 1)
    for j in range(KV_HEADS):
        cols = slice(j * HDIM, (j + 1) * HDIM)
        heads = [slice((j * GROUP + g) * HDIM, (j * GROUP + g + 1) * HDIM) for g in range(GROUP)]
        keys = jnp.concatenate(
            [keys_ref[0, :, cols], far_keys_ref[0, :, cols], chosen(j).astype(bf16)], 0
        )
        values = jnp.concatenate(
            [values_ref[0, :, cols], far_values_ref[0, :, cols], chosen(KV_HEADS + j).astype(bf16)], 0
        )
        query = jnp.concatenate([query_ref[0, :, at] for at in heads], 0)
        grad = jnp.concatenate([grad_ref[0, :, at] for at in heads], 0)
        sink = jnp.concatenate(
            [jnp.full((1, length), sink_ref[j * GROUP + g], f32) for g in range(GROUP)], 1
        )
        score = lax.dot_general(keys, query, NT, preferred_element_type=f32) * scale + bias
        top = jnp.maximum(jnp.max(score, axis=0, keepdims=True), sink)
        weight = jnp.exp(score - top)
        sink_weight = jnp.exp(sink - top)
        inverse = 1.0 / (jnp.sum(weight, axis=0, keepdims=True) + sink_weight)
        prob = weight * inverse
        up = lax.dot_general(values, grad, NT, preferred_element_type=f32)
        delta = jnp.sum(prob * up, axis=0, keepdims=True)
        ds = (prob * (up - delta)).astype(bf16)
        half = prob.astype(bf16)
        sink_row = sink_weight * inverse * delta
        for g in range(GROUP):
            total = jnp.sum(sink_row[:, g * length : (g + 1) * length], axis=1, keepdims=True)
            sinks = sinks - jnp.where(lane == j * GROUP + g, total, 0.0)
        dk = lax.dot_general(ds, query, (((1,), (0,)), ((), ())), preferred_element_type=f32) * scale
        dv = lax.dot_general(half, grad, (((1,), (0,)), ((), ())), preferred_element_type=f32)
        dq = lax.dot_general(keys, ds, TN, preferred_element_type=f32) * scale
        for g in range(GROUP):
            dq_ref[0, :, heads[g]] = jnp.transpose(dq[:, g * length : (g + 1) * length]).astype(bf16)
        wide = KV_HEADS * HDIM
        for base, part in ((0, dk), (wide, dv)):
            at = slice(base + j * HDIM, base + (j + 1) * HDIM)
            own_ref[:, at] = part[:length]
            far_ref[:, at] = part[length : 2 * length].astype(bf16)
        for row, part in ((j, dk), (KV_HEADS + j, dv)):
            for slot in range(slots):
                to_ref = send_ref if slot % 2 else keep_ref
                to_ref[slot // 2, row : row + 1, :] = part[2 * length + slot : 2 * length + slot + 1]
    sinks = jnp.where(iota((8, HDIM), 0) == 0, sinks, 0.0)
    sinks_ref[...] = sinks
    send_ref[slots // 2] = sinks
    keep_ref[slots // 2] = sinks


def last_kernel(row_ref, own_ref, recv_ref, *refs):
    slot_refs, (dk_ref, dv_ref) = refs[:-2], refs[-2:]
    length = own_ref.shape[0]
    slot = slot_refs[0][...]
    for more in slot_refs[1:]:
        slot = slot + more[...]
    mine = iota((length, HDIM), 0) == row_ref[0, 0]
    for out_ref, base in ((dk_ref, 0), (dv_ref, KV_HEADS)):
        for j in range(KV_HEADS):
            at = slice((base + j) * HDIM, (base + j + 1) * HDIM)
            total = own_ref[:, at] + recv_ref[:, at].astype(f32)
            total = total + jnp.where(mine, slot[base + j : base + j + 1, :], 0.0)
            out_ref[0, :, j * HDIM : (j + 1) * HDIM] = total.astype(bf16)


def on_device(
    query_rows, key_rows, value_rows, grad_rows, bucket_rank, sample_rows, sample_count, sink_logit
):
    length = query_rows.shape[1]
    wide = KV_HEADS * HDIM
    slots = lax.axis_size("ctx")
    far_keys = moved(key_rows, "ctx", 1)
    far_values = moved(value_rows, "ctx", 1)
    packs = pl.pallas_call(
        pack_kernel,
        out_shape=jax.ShapeDtypeStruct((PACK, HDIM), bf16),
        in_specs=[SMEM, SMEM, VMEM, VMEM, VMEM],
        out_specs=VMEM,
        name="pack_sample",
    )(sample_rows, sample_count, key_rows, value_rows, bucket_rank)
    packs = jnp.concatenate([packs, moved(packs, "ctx", 1)], 0)
    for offsets in rounds(slots, 2):
        packs = jnp.concatenate([packs] + [moved(packs, "ctx", d) for d in offsets], 0)
    half = slots // 2
    dq, own, far, keep, send, sinks = pl.pallas_call(
        functools.partial(main_kernel, slots),
        out_shape=[
            jax.ShapeDtypeStruct((1, length, HEADS * HDIM), bf16),
            jax.ShapeDtypeStruct((length, 2 * wide), f32),
            jax.ShapeDtypeStruct((length, 2 * wide), bf16),
            jax.ShapeDtypeStruct((half + 1, 8, HDIM), f32),
            jax.ShapeDtypeStruct((half + 1, 8, HDIM), f32),
            jax.ShapeDtypeStruct((8, HDIM), f32),
        ],
        in_specs=[VMEM] * 7 + [SMEM],
        out_specs=[VMEM] * 6,
        compiler_params=pltpu.CompilerParams(vmem_limit_bytes=24 * 1024 * 1024),
        name="attend",
    )(query_rows, grad_rows, key_rows, value_rows, far_keys, far_values, packs, sink_logit)
    terms = keep + moved(send, "ctx", 1)
    recv = moved(far, "ctx", 1)
    slots_left = half
    pieces = [terms[:half], terms[half]]
    for offsets in rounds(slots, 2):
        parts = len(offsets) + 1
        blocks, sinks = pieces
        blocks = blocks.reshape(blocks.shape[0] // parts, parts, 8, HDIM)
        arrived = [
            moved(jnp.concatenate([blocks[:, i + 1], sinks[None]], 0), "ctx", d)
            for i, d in enumerate(offsets)
        ]
        blocks = blocks[:, 0]
        if parts == 4:
            blocks = (blocks + arrived[0][:-1]) + (arrived[1][:-1] + arrived[2][:-1])
            sinks = (sinks + arrived[0][-1]) + (arrived[1][-1] + arrived[2][-1])
        else:
            blocks = blocks + arrived[0][:-1]
            sinks = sinks + arrived[0][-1]
        pieces = [blocks, sinks]
    slot, sinks = pieces
    dk, dv = pl.pallas_call(
        last_kernel,
        out_shape=[jax.ShapeDtypeStruct((1, length, wide), bf16)] * 2,
        in_specs=[SMEM] + [VMEM] * 3,
        out_specs=[VMEM] * 2,
        name="add_up",
    )(sample_rows, own, recv, slot[0])
    for offsets in rounds(lax.axis_size("dp"), 1):
        arrived = [moved(sinks, "dp", d) for d in offsets]
        if len(offsets) == 3:
            sinks = (sinks + arrived[0]) + (arrived[1] + arrived[2])
        else:
            sinks = sinks + arrived[0]
    return dq, dk, dv, sinks[0, :HEADS]


def solution(mesh):
    return jax.shard_map(
        on_device,
        mesh=mesh,
        in_specs=(
            P("dp", "ctx", None),
            P("dp", "ctx", None),
            P("dp", "ctx", None),
            P("dp", "ctx", None),
            P("dp", "ctx"),
            P("dp", "ctx"),
            P("dp", "ctx"),
            P(),
        ),
        out_specs=(P("dp", "ctx", None), P("dp", "ctx", None), P("dp", "ctx", None), P()),
        check_vma=False,
    )
```

```python
import functools

import jax
import jax.numpy as jnp
from jax import lax
from jax.experimental import pallas as pl
from jax.experimental.pallas import tpu as pltpu
from jax.sharding import PartitionSpec as P

HEADS = 16
KV_HEADS = 4
HDIM = 128
BUCKET = 128
GROUP = HEADS // KV_HEADS
NEG = -1e30
PACK = 16
COUNT_ROW = 8
MARK_ROW = 9
TOKEN_MARK_ROW = 10
SINK_ROW = 8

f32 = jnp.float32
bf16 = jnp.bfloat16
NT = (((1,), (1,)), ((), ()))
TN = (((0,), (0,)), ((), ()))
VMEM = pl.BlockSpec(memory_space=pltpu.VMEM)
SMALL = pltpu.CompilerParams(vmem_limit_bytes=6 * 1024 * 1024)


def moved(array, axis, apart):
    return lax.ppermute(array, axis, [(i, i ^ apart) for i in range(lax.axis_size(axis))])


def rounds(size, first):
    found, base = [], first
    while base < size:
        found.append([base] if base * 2 >= size else [base, 2 * base, 3 * base])
        base *= 2 if base * 2 >= size else 4
    return found


def iota(shape, dim):
    return lax.broadcasted_iota(jnp.int32, shape, dim)


def pack_kernel(row_ref, count_ref, keys_ref, values_ref, rank_ref, out_ref):
    length = keys_ref.shape[1]
    row = row_ref[...]
    pick = (iota((PACK, length), 1) == row).astype(bf16)
    key = jnp.dot(pick, keys_ref[0], preferred_element_type=f32)
    value = jnp.dot(pick, values_ref[0], preferred_element_type=f32)
    marks = (rank_ref[...] >= BUCKET).astype(f32)
    lanes = iota((1, length), 1)
    mark = jnp.sum(jnp.where(lanes == row, marks, 0.0), axis=1, keepdims=True)
    rows = iota((PACK, HDIM), 0)
    tile = jnp.zeros((PACK, HDIM), f32)
    for j in range(KV_HEADS):
        tile = jnp.where(rows == j, key[:, j * HDIM : (j + 1) * HDIM], tile)
        tile = jnp.where(rows == KV_HEADS + j, value[:, j * HDIM : (j + 1) * HDIM], tile)
    tile = jnp.where(rows == COUNT_ROW, count_ref[...].astype(f32), tile)
    tile = jnp.where(rows == MARK_ROW, mark, tile)
    tile = jnp.where(rows == TOKEN_MARK_ROW, marks, tile)
    out_ref[...] = tile.astype(bf16)


def main_kernel(
    slots, query_ref, grad_ref, keys_ref, values_ref, far_keys_ref, far_values_ref, packs_ref, sink_ref,
    dq_ref, own_ref, far_ref, out_ref,
):
    length = query_ref.shape[1]
    padded = -(-slots // 16) * 16
    scale = HDIM**-0.5
    packs = packs_ref[...]

    def chosen(row):
        at = iota((padded, slots * PACK), 1)
        slot = iota((padded, slots * PACK), 0)
        return jnp.dot(
            (at == slot * PACK + row).astype(bf16), packs, preferred_element_type=f32
        )

    own_marks = packs[TOKEN_MARK_ROW : TOKEN_MARK_ROW + 1, :].astype(f32)
    far_marks = packs[PACK + TOKEN_MARK_ROW : PACK + TOKEN_MARK_ROW + 1, :].astype(f32)
    own_column = jnp.transpose(jnp.broadcast_to(own_marks, (length, length)))
    far_column = jnp.transpose(jnp.broadcast_to(far_marks, (length, length)))
    slot_at = iota((padded, length), 0)
    slot_bias = jnp.log(jnp.maximum(chosen(COUNT_ROW), 1.0))
    same = (slot_at < 2) & (chosen(MARK_ROW) == own_marks)
    slot_bias = jnp.where(same | (slot_at >= slots), NEG, slot_bias)
    bias = jnp.concatenate(
        [
            jnp.where(own_column == own_marks, 0.0, NEG),
            jnp.where(far_column == own_marks, 0.0, NEG),
            slot_bias,
        ],
        0,
    )
    bias = jnp.concatenate([bias] * GROUP, 1)
    sinks = jnp.zeros((1, HDIM), f32)
    lane = iota((1, HDIM), 1)
    terms = []
    for j in range(KV_HEADS):
        cols = slice(j * HDIM, (j + 1) * HDIM)
        heads = [slice((j * GROUP + g) * HDIM, (j * GROUP + g + 1) * HDIM) for g in range(GROUP)]
        keys = jnp.concatenate(
            [keys_ref[0, :, cols], far_keys_ref[0, :, cols], chosen(j).astype(bf16)], 0
        )
        values = jnp.concatenate(
            [values_ref[0, :, cols], far_values_ref[0, :, cols], chosen(KV_HEADS + j).astype(bf16)], 0
        )
        query = jnp.concatenate([query_ref[0, :, at] for at in heads], 0)
        grad = jnp.concatenate([grad_ref[0, :, at] for at in heads], 0)
        sink = jnp.concatenate(
            [jnp.broadcast_to(sink_ref[:, j * GROUP + g : j * GROUP + g + 1], (1, length)) for g in range(GROUP)], 1
        )
        score = lax.dot_general(keys, query, NT, preferred_element_type=f32) * scale + bias
        top = jnp.maximum(jnp.max(score, axis=0, keepdims=True), sink)
        weight = jnp.exp(score - top)
        sink_weight = jnp.exp(sink - top)
        inverse = 1.0 / (jnp.sum(weight, axis=0, keepdims=True) + sink_weight)
        prob = weight * inverse
        up = lax.dot_general(values, grad, NT, preferred_element_type=f32)
        delta = jnp.sum(prob * up, axis=0, keepdims=True)
        ds = (prob * (up - delta)).astype(bf16)
        half = prob.astype(bf16)
        sink_row = sink_weight * inverse * delta
        for g in range(GROUP):
            total = jnp.sum(sink_row[:, g * length : (g + 1) * length], axis=1, keepdims=True)
            sinks = sinks - jnp.where(lane == j * GROUP + g, total, 0.0)
        dk = lax.dot_general(ds, query, (((1,), (0,)), ((), ())), preferred_element_type=f32) * scale
        dv = lax.dot_general(half, grad, (((1,), (0,)), ((), ())), preferred_element_type=f32)
        dq = lax.dot_general(keys, ds, TN, preferred_element_type=f32) * scale
        for g in range(GROUP):
            dq_ref[0, :, heads[g]] = jnp.transpose(dq[:, g * length : (g + 1) * length]).astype(bf16)
        wide = KV_HEADS * HDIM
        for base, part in ((0, dk), (wide, dv)):
            at = slice(base + j * HDIM, base + (j + 1) * HDIM)
            own_ref[:, at] = part[:length]
            far_ref[:, at] = part[length : 2 * length].astype(bf16)
        terms.append((dk[2 * length :], dv[2 * length :]))
    high = sinks.astype(bf16).astype(f32)
    middle = (sinks - high).astype(bf16).astype(f32)
    low = sinks - high - middle
    rows = iota((PACK, HDIM), 0)
    tile = jnp.zeros((PACK, HDIM), f32)
    for i, part in enumerate((high, middle, low)):
        tile = jnp.where(rows == SINK_ROW + i, part, tile)
    out_ref[...] = jnp.broadcast_to(tile.astype(bf16)[None], out_ref.shape)
    first = lax.axis_index("dp") * slots
    for slot in range(slots):
        mine = tile
        for j in range(KV_HEADS):
            for row, part in zip((j, KV_HEADS + j), terms[j]):
                mine = jnp.where(rows == row, part[slot : slot + 1], mine)
        out_ref[first + (lax.axis_index("ctx") ^ slot)] = mine.astype(bf16)


def last_kernel(slots, row_ref, own_ref, recv_ref, terms_ref, dk_ref, dv_ref, sink_ref):
    length = own_ref.shape[0]
    parts = jnp.sum(terms_ref[...].astype(f32), axis=0)
    sink = parts[SINK_ROW : SINK_ROW + 1] + parts[SINK_ROW + 1 : SINK_ROW + 2]
    sink_ref[...] = (sink + parts[SINK_ROW + 2 : SINK_ROW + 3])[:, :HEADS]
    first = lax.axis_index("dp") * slots
    slot = jnp.sum(terms_ref[pl.ds(first, slots)].astype(f32), axis=0)
    mine = iota((length, HDIM), 0) == row_ref[...]
    for out_ref, base in ((dk_ref, 0), (dv_ref, KV_HEADS)):
        for j in range(KV_HEADS):
            at = slice((base + j) * HDIM, (base + j + 1) * HDIM)
            total = own_ref[:, at] + recv_ref[:, at].astype(f32)
            total = total + jnp.where(mine, slot[base + j : base + j + 1, :], 0.0)
            out_ref[0, :, j * HDIM : (j + 1) * HDIM] = total.astype(bf16)


def on_device(
    query_rows, key_rows, value_rows, grad_rows, bucket_rank, sample_rows, sample_count, sink_logit
):
    length = query_rows.shape[1]
    wide = KV_HEADS * HDIM
    slots = lax.axis_size("ctx")
    far_keys = moved(key_rows, "ctx", 1)
    far_values = moved(value_rows, "ctx", 1)
    packs = pl.pallas_call(
        pack_kernel,
        out_shape=jax.ShapeDtypeStruct((PACK, HDIM), bf16),
        in_specs=[VMEM] * 5,
        out_specs=VMEM,
        compiler_params=SMALL,
        name="pack_sample",
    )(sample_rows, sample_count, key_rows, value_rows, bucket_rank)
    packs = jnp.concatenate([packs, moved(packs, "ctx", 1)], 0)
    for offsets in rounds(slots, 2):
        packs = jnp.concatenate([packs] + [moved(packs, "ctx", d) for d in offsets], 0)
    devices = slots * lax.axis_size("dp")
    dq, own, far, terms = pl.pallas_call(
        functools.partial(main_kernel, slots),
        out_shape=[
            jax.ShapeDtypeStruct((1, length, HEADS * HDIM), bf16),
            jax.ShapeDtypeStruct((length, 2 * wide), f32),
            jax.ShapeDtypeStruct((length, 2 * wide), bf16),
            jax.ShapeDtypeStruct((devices, PACK, HDIM), bf16),
        ],
        in_specs=[VMEM] * 8,
        out_specs=[VMEM] * 4,
        compiler_params=pltpu.CompilerParams(vmem_limit_bytes=24 * 1024 * 1024),
        name="attend",
    )(query_rows, grad_rows, key_rows, value_rows, far_keys, far_values, packs, sink_logit[None])
    recv = moved(far, "ctx", 1)
    terms = lax.all_to_all(terms, ("dp", "ctx"), 0, 0, tiled=True)
    dk, dv, sink_grad = pl.pallas_call(
        functools.partial(last_kernel, slots),
        out_shape=[jax.ShapeDtypeStruct((1, length, wide), bf16)] * 2
        + [jax.ShapeDtypeStruct((1, HEADS), f32)],
        in_specs=[VMEM] * 4,
        out_specs=[VMEM] * 3,
        compiler_params=SMALL,
        name="add_up",
    )(sample_rows, own, recv, terms)
    return dq, dk, dv, sink_grad[0]


def solution(mesh):
    return jax.shard_map(
        on_device,
        mesh=mesh,
        in_specs=(
            P("dp", "ctx", None),
            P("dp", "ctx", None),
            P("dp", "ctx", None),
            P("dp", "ctx", None),
            P("dp", "ctx"),
            P("dp", "ctx"),
            P("dp", "ctx"),
            P(),
        ),
        out_specs=(P("dp", "ctx", None), P("dp", "ctx", None), P("dp", "ctx", None), P()),
        check_vma=False,
    )
```

```python
import functools

import jax
import jax.numpy as jnp
from jax import lax
from jax.experimental import pallas as pl
from jax.experimental.pallas import tpu as pltpu
from jax.sharding import PartitionSpec as P

HEADS = 16
KV_HEADS = 4
HDIM = 128
BUCKET = 128
GROUP = HEADS // KV_HEADS
NEG = -1e30
PACK = 16
COUNT_ROW = 8
MARK_ROW = 9
TOKEN_MARK_ROW = 10
SINK_ROW = 8

f32 = jnp.float32
bf16 = jnp.bfloat16
NN = (((1,), (0,)), ((), ()))
NT = (((1,), (1,)), ((), ()))
TN = (((0,), (0,)), ((), ()))
VMEM = pl.BlockSpec(memory_space=pltpu.VMEM)
SMEM = pl.BlockSpec(memory_space=pltpu.SMEM)
HBM = pl.BlockSpec(memory_space=pltpu.HBM)
LARGE = pltpu.CompilerParams(vmem_limit_bytes=24 * 1024 * 1024)
SMALL = pltpu.CompilerParams(vmem_limit_bytes=6 * 1024 * 1024)


def in_hbm(*arrays):
    return [pltpu.with_memory_space_constraint(array, pltpu.HBM) for array in arrays]


def moved(array, axis, apart):
    return lax.ppermute(array, axis, [(i, i ^ apart) for i in range(lax.axis_size(axis))])


def rounds(size):
    found, base = [], 2
    while base < size:
        found.append([base + 1] if base * 2 >= size else [base + 1, 2 * base + 1, 3 * base + 1])
        base *= 2 if base * 2 >= size else 4
    return found


def slot_order(size):
    order = [0, 1]
    for offsets in rounds(size):
        order = order + [d ^ near for d in offsets for near in order]
    return order


def iota(shape, dim):
    return lax.broadcasted_iota(jnp.int32, shape, dim)


def pack_kernel(
    row_ref, count_ref, rank_hbm, sink_hbm, keys_hbm, values_hbm, query_hbm, grad_hbm,
    kv_ref, qg_ref, out_ref, meta_ref, rank_ref, sink_ref, sems,
):
    wide = keys_hbm.shape[2]
    rows = query_hbm.shape[2]
    copies = [
        pltpu.make_async_copy(from_ref, to_ref, sems.at[i])
        for i, (from_ref, to_ref) in enumerate(
            [
                (keys_hbm.at[0], kv_ref.at[:, :wide]),
                (values_hbm.at[0], kv_ref.at[:, wide:]),
                (rank_hbm, rank_ref),
                (sink_hbm, sink_ref),
                (query_hbm.at[0], qg_ref.at[:, :rows]),
                (grad_hbm.at[0], qg_ref.at[:, rows:]),
            ]
        )
    ]
    for copy in copies:
        copy.start()
    for copy in copies[:4]:
        copy.wait()
    length = kv_ref.shape[0]
    row = row_ref[0, 0]
    pick = (iota((PACK, length), 1) == row).astype(bf16)
    picked = jnp.dot(pick, kv_ref[...], preferred_element_type=f32)
    marks = (rank_ref[...] >= BUCKET).astype(f32)
    mark = jnp.sum(jnp.where(iota((1, length), 1) == row, marks, 0.0), axis=1, keepdims=True)
    at = iota((PACK, HDIM), 0)
    tile = jnp.zeros((PACK, HDIM), f32)
    for j in range(2 * KV_HEADS):
        tile = jnp.where(at == j, picked[:, j * HDIM : (j + 1) * HDIM], tile)
    tile = jnp.where(at == COUNT_ROW, count_ref[0, 0].astype(f32), tile)
    tile = jnp.where(at == MARK_ROW, mark, tile)
    tile = jnp.where(at == TOKEN_MARK_ROW, marks, tile)
    out_ref[...] = tile.astype(bf16)
    at = iota((8, length), 0)
    meta = jnp.where(at == 0, row.astype(f32), 0.0)
    for h in range(HEADS):
        meta = jnp.where((at == 1) & (iota((8, length), 1) == h), sink_ref[:, h : h + 1], meta)
    meta_ref[...] = meta
    for copy in copies[4:]:
        copy.wait()


def columns(j):
    return slice(j * HDIM, (j + 1) * HDIM)


def stacked(qg_ref, base, j):
    heads = [base + j * GROUP + g for g in range(GROUP)]
    return jnp.concatenate([qg_ref[:, columns(h)] for h in heads], 0)


def score_kernel(qg_ref, kv_ref, own_tile_ref, tile_ref, weight_ref, up_ref, stats_ref):
    length = kv_ref.shape[0]
    scale = HDIM**-0.5
    own_marks = own_tile_ref[...].astype(f32)[TOKEN_MARK_ROW : TOKEN_MARK_ROW + 1]
    marks = tile_ref[...].astype(f32)[TOKEN_MARK_ROW : TOKEN_MARK_ROW + 1]
    column = jnp.transpose(jnp.broadcast_to(marks, (length, length)))
    bias = jnp.where(column == own_marks, 0.0, NEG)
    bias = jnp.concatenate([bias] * GROUP, 1)
    for j in range(KV_HEADS):
        at = slice(j * GROUP * HDIM, (j + 1) * GROUP * HDIM)
        score = lax.dot_general(kv_ref[:, columns(j)], stacked(qg_ref, 0, j), NT, preferred_element_type=f32)
        score = score * scale + bias
        top = jnp.max(score, axis=0, keepdims=True)
        weight = jnp.exp(score - top)
        weight_ref[:, at] = weight
        stats_ref[0:1, at] = top
        stats_ref[1:2, at] = jnp.sum(weight, axis=0, keepdims=True)
        up_ref[:, at] = lax.dot_general(
            kv_ref[:, columns(KV_HEADS + j)], stacked(qg_ref, HEADS, j), NT, preferred_element_type=f32
        )


def main_kernel(
    slots, qg_ref, own_weight_ref, own_up_ref, own_stats_ref, far_weight_ref, far_up_ref, far_stats_ref,
    kv_ref, far_ref, packs_ref, meta_ref, dq_hbm, own_grad_ref, far_grad_ref, out_ref, dq_ref, sems,
):
    length = kv_ref.shape[0]
    rows = HEADS * HDIM
    group = GROUP * HDIM
    padded = -(-slots // 16) * 16
    order = slot_order(slots)
    scale = HDIM**-0.5
    packs = packs_ref[...]
    at = iota((padded, slots * PACK), 1)
    slot = iota((padded, slots * PACK), 0)
    pick = jnp.concatenate([(at == slot * PACK + row).astype(bf16) for row in range(MARK_ROW + 1)], 0)
    picked = jnp.dot(pick, packs, preferred_element_type=f32)
    chosen = [picked[i * padded : (i + 1) * padded] for i in range(MARK_ROW + 1)]
    slot_keys = [part.astype(bf16) for part in chosen[:KV_HEADS]]
    slot_values = [part.astype(bf16) for part in chosen[KV_HEADS : 2 * KV_HEADS]]
    own_marks = packs[:PACK].astype(f32)[TOKEN_MARK_ROW : TOKEN_MARK_ROW + 1]
    slot_at = iota((padded, length), 0)
    bias = jnp.log(jnp.maximum(chosen[COUNT_ROW], 1.0))
    same = (slot_at < 2) & (chosen[MARK_ROW] == own_marks)
    bias = jnp.where(same | (slot_at >= slots), NEG, bias)
    sink = jnp.concatenate(
        [jnp.broadcast_to(meta_ref[1:2, h : h + 1], (1, length)) for h in range(HEADS)], 1
    )
    query = [stacked(qg_ref, 0, j) for j in range(KV_HEADS)]
    grad = [stacked(qg_ref, HEADS, j) for j in range(KV_HEADS)]
    score = jnp.concatenate(
        [lax.dot_general(slot_keys[j], query[j], NT, preferred_element_type=f32) for j in range(KV_HEADS)], 1
    )
    slot_up = jnp.concatenate(
        [lax.dot_general(slot_values[j], grad[j], NT, preferred_element_type=f32) for j in range(KV_HEADS)], 1
    )
    score = score * scale + jnp.concatenate([bias] * HEADS, 1)
    own_top, far_top = own_stats_ref[0:1], far_stats_ref[0:1]
    top = jnp.maximum(jnp.maximum(own_top, far_top), jnp.maximum(jnp.max(score, axis=0, keepdims=True), sink))
    slot_weight = jnp.exp(score - top)
    sink_weight = jnp.exp(sink - top)
    own_scale, far_scale = jnp.exp(own_top - top), jnp.exp(far_top - top)
    total = own_scale * own_stats_ref[1:2] + far_scale * far_stats_ref[1:2]
    total = total + (jnp.sum(slot_weight, axis=0, keepdims=True) + sink_weight)
    inverse = 1.0 / total
    own_scale, far_scale = own_scale * inverse, far_scale * inverse
    slot_prob = slot_weight * inverse
    sink_prob = sink_weight * inverse
    slot_delta = jnp.sum(slot_prob * slot_up, axis=0, keepdims=True)
    sinks = jnp.zeros((1, HDIM), f32)
    lane = iota((1, HDIM), 1)
    sent = []
    halves = []
    signals = []
    for j in range(KV_HEADS):
        at = slice(j * group, (j + 1) * group)
        own_prob = own_weight_ref[:, at] * own_scale[:, at]
        far_prob = far_weight_ref[:, at] * far_scale[:, at]
        own_up, far_up = own_up_ref[:, at], far_up_ref[:, at]
        delta = jnp.sum(own_prob * own_up + far_prob * far_up, axis=0, keepdims=True) + slot_delta[:, at]
        ds = jnp.concatenate(
            [
                (own_prob * (own_up - delta)).astype(bf16),
                (far_prob * (far_up - delta)).astype(bf16),
                (slot_prob[:, at] * (slot_up[:, at] - delta)).astype(bf16),
            ],
            0,
        )
        half = jnp.concatenate(
            [own_prob.astype(bf16), far_prob.astype(bf16), slot_prob[:, at].astype(bf16)], 0
        )
        sink_row = sink_prob[:, at] * delta
        for g in range(GROUP):
            part = jnp.sum(sink_row[:, g * length : (g + 1) * length], axis=1, keepdims=True)
            sinks = sinks - jnp.where(lane == j * GROUP + g, part, 0.0)
        keys = jnp.concatenate([kv_ref[:, columns(j)], far_ref[:, columns(j)], slot_keys[j]], 0)
        dq = (lax.dot_general(keys, ds, TN, preferred_element_type=f32) * scale).astype(bf16)
        for g in range(GROUP):
            dq_ref[:, columns(j * GROUP + g)] = jnp.transpose(dq[:, g * length : (g + 1) * length])
        copy = pltpu.make_async_copy(
            dq_ref.at[:, pl.ds(j * group, group)], dq_hbm.at[0, :, pl.ds(j * group, group)], sems.at[j]
        )
        copy.start()
        sent.append(copy)
        halves.append(half)
        signals.append(ds)
    high = sinks.astype(bf16).astype(f32)
    middle = (sinks - high).astype(bf16).astype(f32)
    low = sinks - high - middle
    at = iota((PACK, HDIM), 0)
    tile = jnp.zeros((PACK, HDIM), f32)
    for i, part in enumerate((high, middle, low)):
        tile = jnp.where(at == SINK_ROW + i, part, tile)
    out_ref[...] = jnp.broadcast_to(tile.astype(bf16)[None], out_ref.shape)
    tiles = [tile] * slots
    for j in range(KV_HEADS):
        dk = lax.dot_general(signals[j], query[j], NN, preferred_element_type=f32) * scale
        dv = lax.dot_general(halves[j], grad[j], NN, preferred_element_type=f32)
        for to, part in ((j, dk), (KV_HEADS + j, dv)):
            own_grad_ref[:, columns(to)] = part[:length]
            far_grad_ref[:, columns(to)] = part[length : 2 * length].astype(bf16)
            for slot in range(slots):
                row = part[2 * length + slot : 2 * length + slot + 1]
                tiles[slot] = jnp.where(at == to, row, tiles[slot])
    first = lax.axis_index("dp") * slots
    for slot in range(slots):
        out_ref[first + (lax.axis_index("ctx") ^ order[slot])] = tiles[slot].astype(bf16)
    for copy in sent:
        copy.wait()


def last_kernel(slots, meta_ref, own_ref, recv_ref, terms_ref, dk_ref, dv_ref, sink_ref):
    length = own_ref.shape[0]
    parts = jnp.sum(terms_ref[...].astype(f32), axis=0)
    sink = parts[SINK_ROW : SINK_ROW + 1] + parts[SINK_ROW + 1 : SINK_ROW + 2]
    sink_ref[...] = (sink + parts[SINK_ROW + 2 : SINK_ROW + 3])[:, :HEADS]
    first = lax.axis_index("dp") * slots
    slot = jnp.sum(terms_ref[pl.ds(first, slots)].astype(f32), axis=0)
    mine = iota((length, HDIM), 0).astype(f32) == meta_ref[0:1]
    for out_ref, base in ((dk_ref, 0), (dv_ref, KV_HEADS)):
        for j in range(KV_HEADS):
            at = slice((base + j) * HDIM, (base + j + 1) * HDIM)
            total = own_ref[:, at] + recv_ref[:, at].astype(f32)
            total = total + jnp.where(mine, slot[base + j : base + j + 1, :], 0.0)
            out_ref[0, :, j * HDIM : (j + 1) * HDIM] = total.astype(bf16)


def on_device(
    query_rows, key_rows, value_rows, grad_rows, bucket_rank, sample_rows, sample_count, sink_logit
):
    length = query_rows.shape[1]
    wide = KV_HEADS * HDIM
    slots = lax.axis_size("ctx")
    rows = HEADS * HDIM
    kv, qg, tile, meta = pl.pallas_call(
        pack_kernel,
        out_shape=[
            jax.ShapeDtypeStruct((length, 2 * wide), bf16),
            jax.ShapeDtypeStruct((length, 2 * rows), bf16),
            jax.ShapeDtypeStruct((PACK, HDIM), bf16),
            jax.ShapeDtypeStruct((8, length), f32),
        ],
        in_specs=[SMEM] * 2 + [HBM] * 6,
        out_specs=[VMEM] * 4,
        scratch_shapes=[
            pltpu.VMEM((1, length), jnp.int32),
            pltpu.VMEM((1, HEADS), f32),
            pltpu.SemaphoreType.DMA((6,)),
        ],
        compiler_params=SMALL,
        name="pack_sample",
    )(
        sample_rows,
        sample_count,
        *in_hbm(bucket_rank, sink_logit[None], key_rows, value_rows, query_rows, grad_rows),
    )

    def scores(keys_values, keys_tile):
        return pl.pallas_call(
            score_kernel,
            out_shape=[
                jax.ShapeDtypeStruct((length, rows), f32),
                jax.ShapeDtypeStruct((length, rows), f32),
                jax.ShapeDtypeStruct((8, rows), f32),
            ],
            in_specs=[VMEM] * 4,
            out_specs=[VMEM] * 3,
            compiler_params=LARGE,
            cost_estimate=pl.CostEstimate(
                flops=4 * length * length * rows, transcendentals=length * rows, bytes_accessed=10 * length * rows
            ),
            name="scores",
        )(qg, keys_values, tile, keys_tile)

    far_tile = moved(tile, "ctx", 1)
    far_kv = moved(kv, "ctx", 1)
    own_weight, own_up, own_stats = scores(kv, tile)
    far_weight, far_up, far_stats = scores(far_kv, far_tile)
    packs = jnp.concatenate([tile, far_tile], 0)
    for offsets in rounds(slots):
        packs = jnp.concatenate([packs] + [moved(packs, "ctx", d) for d in offsets], 0)
    devices = slots * lax.axis_size("dp")
    dq, own, far, terms = pl.pallas_call(
        functools.partial(main_kernel, slots),
        out_shape=[
            jax.ShapeDtypeStruct((1, length, rows), bf16),
            jax.ShapeDtypeStruct((length, 2 * wide), f32),
            jax.ShapeDtypeStruct((length, 2 * wide), bf16),
            jax.ShapeDtypeStruct((devices, PACK, HDIM), bf16),
        ],
        in_specs=[VMEM] * 11,
        out_specs=[HBM] + [VMEM] * 3,
        scratch_shapes=[pltpu.VMEM((length, rows), bf16), pltpu.SemaphoreType.DMA((KV_HEADS,))],
        compiler_params=LARGE,
        name="gradients",
    )(qg, own_weight, own_up, own_stats, far_weight, far_up, far_stats, kv, far_kv, packs, meta)
    recv = moved(far, "ctx", 1)
    terms = lax.all_to_all(terms, ("dp", "ctx"), 0, 0, tiled=True)
    dk, dv, sink_grad = pl.pallas_call(
        functools.partial(last_kernel, slots),
        out_shape=[jax.ShapeDtypeStruct((1, length, wide), bf16)] * 2
        + [jax.ShapeDtypeStruct((1, HEADS), f32)],
        in_specs=[VMEM] * 4,
        out_specs=[VMEM] * 3,
        compiler_params=SMALL,
        name="add_up",
    )(meta, own, recv, terms)
    return dq, dk, dv, sink_grad[0]


def solution(mesh):
    return jax.shard_map(
        on_device,
        mesh=mesh,
        in_specs=(
            P("dp", "ctx", None),
            P("dp", "ctx", None),
            P("dp", "ctx", None),
            P("dp", "ctx", None),
            P("dp", "ctx"),
            P("dp", "ctx"),
            P("dp", "ctx"),
            P(),
        ),
        out_specs=(P("dp", "ctx", None), P("dp", "ctx", None), P("dp", "ctx", None), P()),
        check_vma=False,
    )
```

```python
import functools

import jax
import jax.numpy as jnp
from jax import lax
from jax.experimental import pallas as pl
from jax.experimental.pallas import tpu as pltpu
from jax.sharding import PartitionSpec as P

HEADS = 16
KV_HEADS = 4
HDIM = 128
BUCKET = 128
GROUP = HEADS // KV_HEADS
NEG = -1e30
PACK = 16
COUNT_ROW = 8
MARK_ROW = 9
TOKEN_MARK_ROW = 10

f32 = jnp.float32
bf16 = jnp.bfloat16
NN = (((1,), (0,)), ((), ()))
NT = (((1,), (1,)), ((), ()))
TN = (((0,), (0,)), ((), ()))
VMEM = pl.BlockSpec(memory_space=pltpu.VMEM)
SMEM = pl.BlockSpec(memory_space=pltpu.SMEM)
HBM = pl.BlockSpec(memory_space=pltpu.HBM)
LARGE = pltpu.CompilerParams(vmem_limit_bytes=24 * 1024 * 1024)
SMALL = pltpu.CompilerParams(vmem_limit_bytes=6 * 1024 * 1024)


def in_hbm(*arrays):
    return [pltpu.with_memory_space_constraint(array, pltpu.HBM) for array in arrays]


def moved(array, axis, apart):
    return lax.ppermute(array, axis, [(i, i ^ apart) for i in range(lax.axis_size(axis))])


def rounds(size):
    found, base = [], 2
    while base < size:
        found.append([base + 1] if base * 2 >= size else [base + 1, 2 * base + 1, 3 * base + 1])
        base *= 2 if base * 2 >= size else 4
    return found


def slot_order(size):
    order = [0, 1]
    for offsets in rounds(size):
        order = order + [d ^ near for d in offsets for near in order]
    return order


def iota(shape, dim):
    return lax.broadcasted_iota(jnp.int32, shape, dim)


def pack_kernel(
    row_ref, count_ref, rank_hbm, sink_hbm, keys_hbm, values_hbm,
    kv_ref, out_ref, meta_ref, rank_ref, sink_ref, sems,
):
    wide = keys_hbm.shape[2]
    copies = [
        pltpu.make_async_copy(from_ref, to_ref, sems.at[i])
        for i, (from_ref, to_ref) in enumerate(
            [
                (keys_hbm.at[0], kv_ref.at[:, :wide]),
                (values_hbm.at[0], kv_ref.at[:, wide:]),
                (rank_hbm, rank_ref),
                (sink_hbm, sink_ref),
            ]
        )
    ]
    for copy in copies:
        copy.start()
    for copy in copies:
        copy.wait()
    length = kv_ref.shape[0]
    row = row_ref[0, 0]
    pick = (iota((PACK, length), 1) == row).astype(bf16)
    picked = jnp.dot(pick, kv_ref[...], preferred_element_type=f32)
    marks = (rank_ref[...] >= BUCKET).astype(f32)
    mark = jnp.sum(jnp.where(iota((1, length), 1) == row, marks, 0.0), axis=1, keepdims=True)
    at = iota((PACK, HDIM), 0)
    tile = jnp.zeros((PACK, HDIM), f32)
    for j in range(2 * KV_HEADS):
        tile = jnp.where(at == j, picked[:, j * HDIM : (j + 1) * HDIM], tile)
    tile = jnp.where(at == COUNT_ROW, count_ref[0, 0].astype(f32), tile)
    tile = jnp.where(at == MARK_ROW, mark, tile)
    tile = jnp.where(at == TOKEN_MARK_ROW, marks, tile)
    out_ref[...] = tile.astype(bf16)
    at = iota((8, length), 0)
    meta = jnp.where(at == 0, row.astype(f32), 0.0)
    for h in range(HEADS):
        meta = jnp.where((at == 1) & (iota((8, length), 1) == h), sink_ref[:, h : h + 1], meta)
    meta_ref[...] = meta


def columns(j):
    return slice(j * HDIM, (j + 1) * HDIM)


def stacked(ref, j):
    return jnp.concatenate([ref[0, :, columns(j * GROUP + g)] for g in range(GROUP)], 0)


def score_kernel(
    query_ref, grad_ref, kv_ref, far_ref, packs_ref, meta_ref, weight_ref, up_ref, stats_ref, same_ref
):
    same_ref[...] = packs_ref[...]
    length = kv_ref.shape[0]
    scale = HDIM**-0.5
    marks = packs_ref[...].astype(f32)
    own_marks = marks[TOKEN_MARK_ROW : TOKEN_MARK_ROW + 1]
    far_marks = marks[PACK + TOKEN_MARK_ROW : PACK + TOKEN_MARK_ROW + 1]
    own_column = jnp.transpose(jnp.broadcast_to(own_marks, (length, length)))
    far_column = jnp.transpose(jnp.broadcast_to(far_marks, (length, length)))
    bias = jnp.concatenate(
        [jnp.where(own_column == own_marks, 0.0, NEG), jnp.where(far_column == own_marks, 0.0, NEG)], 0
    )
    bias = jnp.concatenate([bias] * GROUP, 1)
    for j in range(KV_HEADS):
        at = slice(j * GROUP * HDIM, (j + 1) * GROUP * HDIM)
        keys = jnp.concatenate([kv_ref[:, columns(j)], far_ref[:, columns(j)]], 0)
        values = jnp.concatenate([kv_ref[:, columns(KV_HEADS + j)], far_ref[:, columns(KV_HEADS + j)]], 0)
        score = lax.dot_general(keys, stacked(query_ref, j), NT, preferred_element_type=f32) * scale + bias
        heads = range(j * GROUP, (j + 1) * GROUP)
        sink = jnp.concatenate([jnp.broadcast_to(meta_ref[1:2, h : h + 1], (1, length)) for h in heads], 1)
        top = jnp.maximum(jnp.max(score, axis=0, keepdims=True), sink)
        weight = jnp.exp(score - top)
        sink_weight = jnp.exp(sink - top)
        weight_ref[:, at] = weight
        up = lax.dot_general(values, stacked(grad_ref, j), NT, preferred_element_type=f32)
        up_ref[:, at] = up
        stats_ref[0:1, at] = top
        stats_ref[1:2, at] = jnp.sum(weight, axis=0, keepdims=True) + sink_weight
        stats_ref[2:3, at] = jnp.sum(weight * up, axis=0, keepdims=True)
        stats_ref[3:4, at] = sink_weight


def main_kernel(
    slots, query_ref, grad_ref, weight_ref, up_ref, stats_ref,
    kv_ref, far_ref, packs_ref, dq_hbm, own_grad_ref, far_grad_ref, out_ref, dq_ref, sinks_ref, sems,
):
    length = kv_ref.shape[0]
    rows = HEADS * HDIM
    group = GROUP * HDIM
    padded = -(-slots // 16) * 16
    order = slot_order(slots)
    scale = HDIM**-0.5
    packs = packs_ref[...]
    at = iota((padded, slots * PACK), 1)
    slot = iota((padded, slots * PACK), 0)
    pick = jnp.concatenate([(at == slot * PACK + row).astype(bf16) for row in range(MARK_ROW + 1)], 0)
    picked = jnp.dot(pick, packs, preferred_element_type=f32)
    chosen = [picked[i * padded : (i + 1) * padded] for i in range(MARK_ROW + 1)]
    slot_keys = [part.astype(bf16) for part in chosen[:KV_HEADS]]
    slot_values = [part.astype(bf16) for part in chosen[KV_HEADS : 2 * KV_HEADS]]
    own_marks = packs[:PACK].astype(f32)[TOKEN_MARK_ROW : TOKEN_MARK_ROW + 1]
    slot_at = iota((padded, length), 0)
    bias = jnp.log(jnp.maximum(chosen[COUNT_ROW], 1.0))
    same = (slot_at < 2) & (chosen[MARK_ROW] == own_marks)
    bias = jnp.where(same | (slot_at >= slots), NEG, bias)
    query = [stacked(query_ref, j) for j in range(KV_HEADS)]
    grad = [stacked(grad_ref, j) for j in range(KV_HEADS)]
    score = jnp.concatenate(
        [lax.dot_general(slot_keys[j], query[j], NT, preferred_element_type=f32) for j in range(KV_HEADS)], 1
    )
    slot_up = jnp.concatenate(
        [lax.dot_general(slot_values[j], grad[j], NT, preferred_element_type=f32) for j in range(KV_HEADS)], 1
    )
    score = score * scale + jnp.concatenate([bias] * HEADS, 1)
    pair_top = stats_ref[0:1]
    top = jnp.maximum(pair_top, jnp.max(score, axis=0, keepdims=True))
    slot_weight = jnp.exp(score - top)
    pair_scale = jnp.exp(pair_top - top)
    inverse = 1.0 / (pair_scale * stats_ref[1:2] + jnp.sum(slot_weight, axis=0, keepdims=True))
    pair_scale = pair_scale * inverse
    slot_prob = slot_weight * inverse
    delta = pair_scale * stats_ref[2:3] + jnp.sum(slot_prob * slot_up, axis=0, keepdims=True)
    slot_ds = (slot_prob * (slot_up - delta)).astype(bf16)
    slot_half = slot_prob.astype(bf16)
    sink_rows = pair_scale * stats_ref[3:4] * delta
    for h in range(HEADS):
        sinks_ref[h : h + 1] = sink_rows[:, h * length : (h + 1) * length]
    sent = []
    halves = []
    signals = []
    for j in range(KV_HEADS):
        at = slice(j * group, (j + 1) * group)
        prob = weight_ref[:, at] * pair_scale[:, at]
        ds = jnp.concatenate([(prob * (up_ref[:, at] - delta[:, at])).astype(bf16), slot_ds[:, at]], 0)
        half = jnp.concatenate([prob.astype(bf16), slot_half[:, at]], 0)
        keys = jnp.concatenate([kv_ref[:, columns(j)], far_ref[:, columns(j)], slot_keys[j]], 0)
        dq = (lax.dot_general(ds, keys, TN, preferred_element_type=f32) * scale).astype(bf16)
        for g in range(GROUP):
            dq_ref[:, columns(j * GROUP + g)] = dq[g * length : (g + 1) * length]
        copy = pltpu.make_async_copy(
            dq_ref.at[:, pl.ds(j * group, group)], dq_hbm.at[0, :, pl.ds(j * group, group)], sems.at[j]
        )
        copy.start()
        sent.append(copy)
        halves.append(half)
        signals.append(ds)
    sinks = jnp.sum(sinks_ref[...], axis=1, keepdims=True)
    sinks = jnp.where(iota((HEADS, HDIM), 0) == iota((HEADS, HDIM), 1), -sinks, 0.0)
    sinks = jnp.sum(sinks, axis=0, keepdims=True)
    high = sinks.astype(bf16).astype(f32)
    ends = (high, sinks - high)
    wide = KV_HEADS * HDIM
    key_rows, value_rows = [], []
    for j in range(KV_HEADS):
        dk = lax.dot_general(signals[j], query[j], NN, preferred_element_type=f32) * scale
        dv = lax.dot_general(halves[j], grad[j], NN, preferred_element_type=f32)
        for to, part, kept in ((j, dk, key_rows), (KV_HEADS + j, dv, value_rows)):
            own_grad_ref[:, columns(to)] = part[:length]
            far_grad_ref[:, columns(to)] = part[length : 2 * length].astype(bf16)
            kept.append(part[2 * length :])

    def piece(first, second):
        shape = out_ref.shape[1:]
        upper = jnp.broadcast_to(jnp.concatenate([first, ends[0]], 1), shape)
        lower = jnp.broadcast_to(jnp.concatenate([second, ends[1]], 1), shape)
        return jnp.where(iota(shape, 0) == 0, upper, lower).astype(bf16)

    nothing = jnp.zeros((1, wide), f32)
    out_ref[...] = jnp.broadcast_to(piece(nothing, nothing)[None], out_ref.shape)
    key_rows = jnp.concatenate(key_rows, 1)
    value_rows = jnp.concatenate(value_rows, 1)
    first = lax.axis_index("dp") * slots
    for slot in range(slots):
        out_ref[first + (lax.axis_index("ctx") ^ order[slot])] = piece(
            key_rows[slot : slot + 1], value_rows[slot : slot + 1]
        )
    for copy in sent:
        copy.wait()


def last_kernel(slots, meta_ref, own_ref, recv_ref, terms_ref, dk_ref, dv_ref, sink_ref):
    length = own_ref.shape[0]
    wide = KV_HEADS * HDIM
    ends = jnp.sum(terms_ref[:, :, wide:].astype(f32), axis=0)
    sink_ref[...] = (ends[0:1] + ends[1:2])[:, :HEADS]
    first = lax.axis_index("dp") * slots
    slot = jnp.sum(terms_ref[pl.ds(first, slots), :, :wide].astype(f32), axis=0)
    mine = iota((length, HDIM), 0).astype(f32) == meta_ref[0:1]
    for i, out_ref in enumerate((dk_ref, dv_ref)):
        for j in range(KV_HEADS):
            at = columns(i * KV_HEADS + j)
            total = own_ref[:, at] + recv_ref[:, at].astype(f32)
            total = total + jnp.where(mine, slot[i : i + 1, columns(j)], 0.0)
            out_ref[0, :, columns(j)] = total.astype(bf16)


def on_device(
    query_rows, key_rows, value_rows, grad_rows, bucket_rank, sample_rows, sample_count, sink_logit
):
    length = query_rows.shape[1]
    wide = KV_HEADS * HDIM
    slots = lax.axis_size("ctx")
    rows = HEADS * HDIM
    kv, tile, meta = pl.pallas_call(
        pack_kernel,
        out_shape=[
            jax.ShapeDtypeStruct((length, 2 * wide), bf16),
            jax.ShapeDtypeStruct((PACK, HDIM), bf16),
            jax.ShapeDtypeStruct((8, length), f32),
        ],
        in_specs=[SMEM] * 2 + [HBM] * 4,
        out_specs=[VMEM] * 3,
        scratch_shapes=[
            pltpu.VMEM((1, length), jnp.int32),
            pltpu.VMEM((1, HEADS), f32),
            pltpu.SemaphoreType.DMA((4,)),
        ],
        compiler_params=SMALL,
        cost_estimate=pl.CostEstimate(flops=10**10, transcendentals=0, bytes_accessed=10**7),
        name="pack_sample",
    )(
        sample_rows,
        sample_count,
        *in_hbm(bucket_rank, sink_logit[None], key_rows, value_rows),
    )

    far_tile = moved(tile, "ctx", 1)
    far_kv = moved(kv, "ctx", 1)
    packs = jnp.concatenate([tile, far_tile], 0)
    weight, up, stats, same = pl.pallas_call(
        score_kernel,
        out_shape=[
            jax.ShapeDtypeStruct((2 * length, rows), f32),
            jax.ShapeDtypeStruct((2 * length, rows), f32),
            jax.ShapeDtypeStruct((8, rows), f32),
            jax.ShapeDtypeStruct(packs.shape, bf16),
        ],
        in_specs=[VMEM] * 6,
        out_specs=[VMEM] * 4,
        compiler_params=LARGE,
        cost_estimate=pl.CostEstimate(
            flops=8 * length * length * rows, transcendentals=2 * length * rows, bytes_accessed=20 * length * rows
        ),
        name="pair_scores",
    )(query_rows, grad_rows, kv, far_kv, packs, meta)
    for offsets in rounds(slots):
        arrived = [moved(packs, "ctx", d) for d in offsets]
        packs = jnp.concatenate([same] + arrived, 0)
        same = packs
    devices = slots * lax.axis_size("dp")
    dq, own, far, terms = pl.pallas_call(
        functools.partial(main_kernel, slots),
        out_shape=[
            jax.ShapeDtypeStruct((1, length, rows), bf16),
            jax.ShapeDtypeStruct((length, 2 * wide), f32),
            jax.ShapeDtypeStruct((length, 2 * wide), bf16),
            jax.ShapeDtypeStruct((devices, 2, wide + HDIM), bf16),
        ],
        in_specs=[VMEM] * 8,
        out_specs=[HBM] + [VMEM] * 3,
        scratch_shapes=[
            pltpu.VMEM((length, rows), bf16),
            pltpu.VMEM((HEADS, length), f32),
            pltpu.SemaphoreType.DMA((KV_HEADS,)),
        ],
        compiler_params=LARGE,
        name="gradients",
    )(query_rows, grad_rows, weight, up, stats, kv, far_kv, packs)
    recv = moved(far, "ctx", 1)
    terms = lax.all_to_all(terms, ("dp", "ctx"), 0, 0, tiled=True)
    dk, dv, sink_grad = pl.pallas_call(
        functools.partial(last_kernel, slots),
        out_shape=[jax.ShapeDtypeStruct((1, length, wide), bf16)] * 2
        + [jax.ShapeDtypeStruct((1, HEADS), f32)],
        in_specs=[VMEM] * 4,
        out_specs=[VMEM] * 3,
        compiler_params=SMALL,
        name="add_up",
    )(meta, own, recv, terms)
    return dq, dk, dv, sink_grad[0]


def solution(mesh):
    return jax.shard_map(
        on_device,
        mesh=mesh,
        in_specs=(
            P("dp", "ctx", None),
            P("dp", "ctx", None),
            P("dp", "ctx", None),
            P("dp", "ctx", None),
            P("dp", "ctx"),
            P("dp", "ctx"),
            P("dp", "ctx"),
            P(),
        ),
        out_specs=(P("dp", "ctx", None), P("dp", "ctx", None), P("dp", "ctx", None), P()),
        check_vma=False,
    )
```

```python
import functools

import jax
import jax.numpy as jnp
from jax import lax
from jax.experimental import pallas as pl
from jax.experimental.pallas import tpu as pltpu
from jax.sharding import PartitionSpec as P

HEADS = 16
KV_HEADS = 4
HDIM = 128
BUCKET = 128
GROUP = HEADS // KV_HEADS
NEG = -1e30
PACK = 16
COUNT_ROW = 8
MARK_ROW = 9
TOKEN_MARK_ROW = 10

f32 = jnp.float32
bf16 = jnp.bfloat16
NN = (((1,), (0,)), ((), ()))
NT = (((1,), (1,)), ((), ()))
TN = (((0,), (0,)), ((), ()))
VMEM = pl.BlockSpec(memory_space=pltpu.VMEM)
SMEM = pl.BlockSpec(memory_space=pltpu.SMEM)
HBM = pl.BlockSpec(memory_space=pltpu.HBM)
LARGE = pltpu.CompilerParams(vmem_limit_bytes=24 * 1024 * 1024)
LOADS = pl.CostEstimate(flops=10**10, transcendentals=0, bytes_accessed=10**7)
SMALL = pltpu.CompilerParams(vmem_limit_bytes=6 * 1024 * 1024)


def in_hbm(*arrays):
    return [pltpu.with_memory_space_constraint(array, pltpu.HBM) for array in arrays]


def moved(array, axis, apart):
    return lax.ppermute(array, axis, [(i, i ^ apart) for i in range(lax.axis_size(axis))])


def rounds(size):
    found, base = [], 2
    while base < size:
        found.append([base + 1] if base * 2 >= size else [base + 1, 2 * base + 1, 3 * base + 1])
        base *= 2 if base * 2 >= size else 4
    return found


def slot_order(size):
    order = [0, 1]
    for offsets in rounds(size):
        order = order + [d ^ near for d in offsets for near in order]
    return order


def iota(shape, dim):
    return lax.broadcasted_iota(jnp.int32, shape, dim)


def token_kernel(out_ref):
    out_ref[...] = iota(out_ref.shape, 1)


def pack_kernel(
    row_ref, count_ref, token_ref, rank_ref, sink_ref, keys_ref, values_ref, kv_ref, out_ref, meta_ref
):
    wide = keys_ref.shape[2]
    kv_ref[:, :wide] = keys_ref[0]
    kv_ref[:, wide:] = values_ref[0]
    length = kv_ref.shape[0]
    row = row_ref[0, 0]
    pick = (token_ref[...] == row).astype(bf16)
    picked = jnp.dot(pick, kv_ref[...], preferred_element_type=f32)
    marks = (rank_ref[...] >= BUCKET).astype(f32)
    mark = jnp.sum(jnp.where(token_ref[:1] == row, marks, 0.0), axis=1, keepdims=True)
    at = iota((PACK, HDIM), 0)
    tile = jnp.zeros((PACK, HDIM), f32)
    for j in range(2 * KV_HEADS):
        tile = jnp.where(at == j, picked[:, j * HDIM : (j + 1) * HDIM], tile)
    tile = jnp.where(at == COUNT_ROW, count_ref[0, 0].astype(f32), tile)
    tile = jnp.where(at == MARK_ROW, mark, tile)
    tile = jnp.where(at == TOKEN_MARK_ROW, marks, tile)
    out_ref[...] = tile.astype(bf16)
    at = iota((8, length), 0)
    meta = jnp.where(at == 0, row.astype(f32), 0.0)
    sinks = jnp.concatenate([sink_ref[...], jnp.zeros((1, length - HEADS), f32)], 1)
    meta = jnp.where(at == 1, sinks, meta)
    meta_ref[...] = meta


def columns(j):
    return slice(j * HDIM, (j + 1) * HDIM)


def stacked(ref, j):
    return jnp.concatenate([ref[0, :, columns(j * GROUP + g)] for g in range(GROUP)], 0)


def score_kernel(
    query_ref, grad_ref, kv_ref, far_ref, packs_ref, meta_ref, weight_ref, up_ref, stats_ref, same_ref
):
    same_ref[...] = packs_ref[...]
    length = kv_ref.shape[0]
    scale = HDIM**-0.5
    marks = packs_ref[...].astype(f32)
    own_marks = marks[TOKEN_MARK_ROW : TOKEN_MARK_ROW + 1]
    far_marks = marks[PACK + TOKEN_MARK_ROW : PACK + TOKEN_MARK_ROW + 1]
    own_column = jnp.transpose(jnp.broadcast_to(own_marks, (length, length)))
    far_column = jnp.transpose(jnp.broadcast_to(far_marks, (length, length)))
    bias = jnp.concatenate(
        [jnp.where(own_column == own_marks, 0.0, NEG), jnp.where(far_column == own_marks, 0.0, NEG)], 0
    )
    bias = jnp.concatenate([bias] * GROUP, 1)
    for j in range(KV_HEADS):
        at = slice(j * GROUP * HDIM, (j + 1) * GROUP * HDIM)
        keys = jnp.concatenate([kv_ref[:, columns(j)], far_ref[:, columns(j)]], 0)
        values = jnp.concatenate([kv_ref[:, columns(KV_HEADS + j)], far_ref[:, columns(KV_HEADS + j)]], 0)
        score = lax.dot_general(keys, stacked(query_ref, j), NT, preferred_element_type=f32) * scale + bias
        heads = range(j * GROUP, (j + 1) * GROUP)
        sink = jnp.concatenate([jnp.broadcast_to(meta_ref[1:2, h : h + 1], (1, length)) for h in heads], 1)
        top = jnp.maximum(jnp.max(score, axis=0, keepdims=True), sink)
        weight = jnp.exp(score - top)
        sink_weight = jnp.exp(sink - top)
        weight_ref[:, at] = weight
        up = lax.dot_general(values, stacked(grad_ref, j), NT, preferred_element_type=f32)
        up_ref[:, at] = up
        stats_ref[0:1, at] = top
        stats_ref[1:2, at] = jnp.sum(weight, axis=0, keepdims=True) + sink_weight
        stats_ref[2:3, at] = jnp.sum(weight * up, axis=0, keepdims=True)
        stats_ref[3:4, at] = sink_weight


def main_kernel(
    slots, query_ref, grad_ref, weight_ref, up_ref, stats_ref,
    kv_ref, far_ref, packs_ref, dq_hbm, own_grad_ref, far_grad_ref, out_ref, dq_ref, sinks_ref, sems,
):
    length = kv_ref.shape[0]
    rows = HEADS * HDIM
    group = GROUP * HDIM
    padded = -(-slots // 16) * 16
    order = slot_order(slots)
    scale = HDIM**-0.5
    packs = packs_ref[...]
    at = iota((padded, slots * PACK), 1)
    slot = iota((padded, slots * PACK), 0)
    pick = jnp.concatenate([(at == slot * PACK + row).astype(bf16) for row in range(MARK_ROW + 1)], 0)
    picked = jnp.dot(pick, packs, preferred_element_type=f32)
    chosen = [picked[i * padded : (i + 1) * padded] for i in range(MARK_ROW + 1)]
    slot_keys = [part.astype(bf16) for part in chosen[:KV_HEADS]]
    slot_values = [part.astype(bf16) for part in chosen[KV_HEADS : 2 * KV_HEADS]]
    own_marks = packs[:PACK].astype(f32)[TOKEN_MARK_ROW : TOKEN_MARK_ROW + 1]
    slot_at = iota((padded, length), 0)
    bias = jnp.log(jnp.maximum(chosen[COUNT_ROW], 1.0))
    same = (slot_at < 2) & (chosen[MARK_ROW] == own_marks)
    bias = jnp.where(same | (slot_at >= slots), NEG, bias)
    query = [stacked(query_ref, j) for j in range(KV_HEADS)]
    grad = [stacked(grad_ref, j) for j in range(KV_HEADS)]
    score = jnp.concatenate(
        [lax.dot_general(slot_keys[j], query[j], NT, preferred_element_type=f32) for j in range(KV_HEADS)], 1
    )
    slot_up = jnp.concatenate(
        [lax.dot_general(slot_values[j], grad[j], NT, preferred_element_type=f32) for j in range(KV_HEADS)], 1
    )
    score = score * scale + jnp.concatenate([bias] * HEADS, 1)
    pair_top = stats_ref[0:1]
    top = jnp.maximum(pair_top, jnp.max(score, axis=0, keepdims=True))
    slot_weight = jnp.exp(score - top)
    pair_scale = jnp.exp(pair_top - top)
    inverse = 1.0 / (pair_scale * stats_ref[1:2] + jnp.sum(slot_weight, axis=0, keepdims=True))
    pair_scale = pair_scale * inverse
    slot_prob = slot_weight * inverse
    delta = pair_scale * stats_ref[2:3] + jnp.sum(slot_prob * slot_up, axis=0, keepdims=True)
    slot_ds = (slot_prob * (slot_up - delta)).astype(bf16)
    slot_half = slot_prob.astype(bf16)
    sink_rows = pair_scale * stats_ref[3:4] * delta
    for h in range(HEADS):
        sinks_ref[h : h + 1] = sink_rows[:, h * length : (h + 1) * length]
    sent = []
    halves = []
    signals = []
    for j in range(KV_HEADS):
        at = slice(j * group, (j + 1) * group)
        prob = weight_ref[:, at] * pair_scale[:, at]
        ds = jnp.concatenate([(prob * (up_ref[:, at] - delta[:, at])).astype(bf16), slot_ds[:, at]], 0)
        half = jnp.concatenate([prob.astype(bf16), slot_half[:, at]], 0)
        keys = jnp.concatenate([kv_ref[:, columns(j)], far_ref[:, columns(j)], slot_keys[j]], 0)
        dq = (lax.dot_general(ds, keys, TN, preferred_element_type=f32) * scale).astype(bf16)
        for g in range(GROUP):
            dq_ref[:, columns(j * GROUP + g)] = dq[g * length : (g + 1) * length]
        copy = pltpu.make_async_copy(
            dq_ref.at[:, pl.ds(j * group, group)], dq_hbm.at[0, :, pl.ds(j * group, group)], sems.at[j]
        )
        copy.start()
        sent.append(copy)
        halves.append(half)
        signals.append(ds)
    sinks = jnp.sum(sinks_ref[...], axis=1, keepdims=True)
    sinks = jnp.where(iota((HEADS, HDIM), 0) == iota((HEADS, HDIM), 1), -sinks, 0.0)
    sinks = jnp.sum(sinks, axis=0, keepdims=True)
    high = sinks.astype(bf16).astype(f32)
    ends = (high, sinks - high)
    wide = KV_HEADS * HDIM
    key_rows, value_rows = [], []
    for j in range(KV_HEADS):
        dk = lax.dot_general(signals[j], query[j], NN, preferred_element_type=f32) * scale
        dv = lax.dot_general(halves[j], grad[j], NN, preferred_element_type=f32)
        for to, part, kept in ((j, dk, key_rows), (KV_HEADS + j, dv, value_rows)):
            own_grad_ref[:, columns(to)] = part[:length]
            far_grad_ref[:, columns(to)] = part[length : 2 * length].astype(bf16)
            kept.append(part[2 * length :])

    def piece(first, second):
        shape = out_ref.shape[1:]
        upper = jnp.broadcast_to(jnp.concatenate([first, ends[0]], 1), shape)
        lower = jnp.broadcast_to(jnp.concatenate([second, ends[1]], 1), shape)
        return jnp.where(iota(shape, 0) == 0, upper, lower).astype(bf16)

    nothing = jnp.zeros((1, wide), f32)
    out_ref[...] = jnp.broadcast_to(piece(nothing, nothing)[None], out_ref.shape)
    key_rows = jnp.concatenate(key_rows, 1)
    value_rows = jnp.concatenate(value_rows, 1)
    first = lax.axis_index("dp") * slots
    for slot in range(slots):
        out_ref[first + (lax.axis_index("ctx") ^ order[slot])] = piece(
            key_rows[slot : slot + 1], value_rows[slot : slot + 1]
        )
    for copy in sent:
        copy.wait()


def last_kernel(slots, meta_ref, own_ref, recv_ref, terms_ref, dk_ref, dv_ref, sink_ref):
    length = own_ref.shape[0]
    wide = KV_HEADS * HDIM
    ends = jnp.sum(terms_ref[:, :, wide:].astype(f32), axis=0)
    sink_ref[...] = (ends[0:1] + ends[1:2])[:, :HEADS]
    first = lax.axis_index("dp") * slots
    slot = jnp.sum(terms_ref[pl.ds(first, slots), :, :wide].astype(f32), axis=0)
    mine = iota((length, HDIM), 0).astype(f32) == meta_ref[0:1]
    for i, out_ref in enumerate((dk_ref, dv_ref)):
        for j in range(KV_HEADS):
            at = columns(i * KV_HEADS + j)
            total = own_ref[:, at] + recv_ref[:, at].astype(f32)
            total = total + jnp.where(mine, slot[i : i + 1, columns(j)], 0.0)
            out_ref[0, :, columns(j)] = total.astype(bf16)


def on_device(
    query_rows, key_rows, value_rows, grad_rows, bucket_rank, sample_rows, sample_count, sink_logit
):
    length = query_rows.shape[1]
    wide = KV_HEADS * HDIM
    slots = lax.axis_size("ctx")
    rows = HEADS * HDIM
    token = pl.pallas_call(
        token_kernel,
        out_shape=jax.ShapeDtypeStruct((PACK, length), jnp.int32),
        out_specs=VMEM,
        compiler_params=SMALL,
        cost_estimate=LOADS,
        name="token_lanes",
    )()
    sample_rows, sample_count, token = lax.optimization_barrier((sample_rows, sample_count, token))
    kv, tile, meta = pl.pallas_call(
        pack_kernel,
        out_shape=[
            jax.ShapeDtypeStruct((length, 2 * wide), bf16),
            jax.ShapeDtypeStruct((PACK, HDIM), bf16),
            jax.ShapeDtypeStruct((8, length), f32),
        ],
        in_specs=[SMEM] * 2 + [VMEM] * 5,
        out_specs=[VMEM] * 3,
        compiler_params=SMALL,
        cost_estimate=LOADS,
        name="pack_sample",
    )(sample_rows, sample_count, token, bucket_rank, sink_logit[None], key_rows, value_rows)

    far_tile = moved(tile, "ctx", 1)
    far_kv = moved(kv, "ctx", 1)
    packs = jnp.concatenate([tile, far_tile], 0)
    weight, up, stats, same = pl.pallas_call(
        score_kernel,
        out_shape=[
            jax.ShapeDtypeStruct((2 * length, rows), f32),
            jax.ShapeDtypeStruct((2 * length, rows), f32),
            jax.ShapeDtypeStruct((8, rows), f32),
            jax.ShapeDtypeStruct(packs.shape, bf16),
        ],
        in_specs=[VMEM] * 6,
        out_specs=[VMEM] * 4,
        compiler_params=LARGE,
        cost_estimate=pl.CostEstimate(
            flops=8 * length * length * rows, transcendentals=2 * length * rows, bytes_accessed=20 * length * rows
        ),
        name="pair_scores",
    )(query_rows, grad_rows, kv, far_kv, packs, meta)
    for offsets in rounds(slots):
        arrived = [moved(packs, "ctx", d) for d in offsets]
        packs = jnp.concatenate([same] + arrived, 0)
        same = packs
    devices = slots * lax.axis_size("dp")
    dq, own, far, terms = pl.pallas_call(
        functools.partial(main_kernel, slots),
        out_shape=[
            jax.ShapeDtypeStruct((1, length, rows), bf16),
            jax.ShapeDtypeStruct((length, 2 * wide), f32),
            jax.ShapeDtypeStruct((length, 2 * wide), bf16),
            jax.ShapeDtypeStruct((devices, 2, wide + HDIM), bf16),
        ],
        in_specs=[VMEM] * 8,
        out_specs=[HBM] + [VMEM] * 3,
        scratch_shapes=[
            pltpu.VMEM((length, rows), bf16),
            pltpu.VMEM((HEADS, length), f32),
            pltpu.SemaphoreType.DMA((KV_HEADS,)),
        ],
        compiler_params=LARGE,
        name="gradients",
    )(query_rows, grad_rows, weight, up, stats, kv, far_kv, packs)
    recv = moved(far, "ctx", 1)
    terms = lax.all_to_all(terms, ("dp", "ctx"), 0, 0, tiled=True)
    dk, dv, sink_grad = pl.pallas_call(
        functools.partial(last_kernel, slots),
        out_shape=[jax.ShapeDtypeStruct((1, length, wide), bf16)] * 2
        + [jax.ShapeDtypeStruct((1, HEADS), f32)],
        in_specs=[VMEM] * 4,
        out_specs=[VMEM] * 3,
        compiler_params=SMALL,
        name="add_up",
    )(meta, own, recv, terms)
    return dq, dk, dv, sink_grad[0]


def solution(mesh):
    return jax.shard_map(
        on_device,
        mesh=mesh,
        in_specs=(
            P("dp", "ctx", None),
            P("dp", "ctx", None),
            P("dp", "ctx", None),
            P("dp", "ctx", None),
            P("dp", "ctx"),
            P("dp", "ctx"),
            P("dp", "ctx"),
            P(),
        ),
        out_specs=(P("dp", "ctx", None), P("dp", "ctx", None), P("dp", "ctx", None), P()),
        check_vma=False,
    )
```

```python
import functools

import jax
import jax.numpy as jnp
from jax import lax
from jax.experimental import pallas as pl
from jax.experimental.pallas import tpu as pltpu
from jax.sharding import PartitionSpec as P

HEADS = 16
KV_HEADS = 4
HDIM = 128
BUCKET = 128
GROUP = HEADS // KV_HEADS
NEG = -1e30
PACK = 16
COUNT_ROW = 8
MARK_ROW = 9
RANK_ROW = 10

f32 = jnp.float32
bf16 = jnp.bfloat16
NN = (((1,), (0,)), ((), ()))
NT = (((1,), (1,)), ((), ()))
TN = (((0,), (0,)), ((), ()))
VMEM = pl.BlockSpec(memory_space=pltpu.VMEM)
SMEM = pl.BlockSpec(memory_space=pltpu.SMEM)
HBM = pl.BlockSpec(memory_space=pltpu.HBM)
LARGE = pltpu.CompilerParams(vmem_limit_bytes=24 * 1024 * 1024)
LOADS = pl.CostEstimate(flops=10**10, transcendentals=0, bytes_accessed=10**7)
SMALL = pltpu.CompilerParams(vmem_limit_bytes=6 * 1024 * 1024)


def in_hbm(*arrays):
    return [pltpu.with_memory_space_constraint(array, pltpu.HBM) for array in arrays]


def moved(array, axis, apart):
    return lax.ppermute(array, axis, [(i, i ^ apart) for i in range(lax.axis_size(axis))])


def rounds(size):
    found, base = [], 2
    while base < size:
        found.append([base + 1] if base * 2 >= size else [base + 1, 2 * base + 1, 3 * base + 1])
        base *= 2 if base * 2 >= size else 4
    return found


def slot_order(size):
    order = [0, 1]
    for offsets in rounds(size):
        order = order + [d ^ near for d in offsets for near in order]
    return order


def iota(shape, dim):
    return lax.broadcasted_iota(jnp.int32, shape, dim)


def token_kernel(out_ref):
    out_ref[...] = iota(out_ref.shape, 1)


def pack_kernel(
    row_ref, count_ref, token_ref, rank_ref, keys_ref, values_ref, kv_ref, out_ref, meta_ref
):
    wide = keys_ref.shape[2]
    kv_ref[:, :wide] = keys_ref[0]
    kv_ref[:, wide:] = values_ref[0]
    length = kv_ref.shape[0]
    row = row_ref[0, 0]
    pick = (token_ref[...] == row).astype(bf16)
    picked = jnp.dot(pick, kv_ref[...], preferred_element_type=f32)
    ranks = rank_ref[...].astype(f32)
    mark = jnp.sum(jnp.where(token_ref[:1] == row, ranks, 0.0), axis=1, keepdims=True)
    mark = (mark >= BUCKET).astype(f32)
    at = iota((PACK, HDIM), 0)
    tile = jnp.zeros((PACK, HDIM), f32)
    for j in range(2 * KV_HEADS):
        tile = jnp.where(at == j, picked[:, j * HDIM : (j + 1) * HDIM], tile)
    tile = jnp.where(at == COUNT_ROW, count_ref[0, 0].astype(f32), tile)
    tile = jnp.where(at == MARK_ROW, mark, tile)
    tile = jnp.where(at == RANK_ROW, ranks, tile)
    out_ref[...] = tile.astype(bf16)
    at = iota((8, length), 0)
    meta = jnp.where(at == 0, row.astype(f32), 0.0)
    meta_ref[...] = meta


def columns(j):
    return slice(j * HDIM, (j + 1) * HDIM)


def stacked(ref, j):
    return jnp.concatenate([ref[0, :, columns(j * GROUP + g)] for g in range(GROUP)], 0)


def by_bucket(rows, first):
    low = jnp.concatenate([first] * GROUP, 0).astype(bf16)
    high = jnp.concatenate([1.0 - first] * GROUP, 0).astype(bf16)
    return jnp.concatenate([rows * low, rows * high], 1)


def score_kernel(
    query_ref, grad_ref, kv_ref, far_ref, packs_ref, sink_ref,
    weight_ref, up_ref, stats_ref, keys2_ref, home_ref, first_ref, same_ref,
):
    same_ref[...] = packs_ref[...]
    length = kv_ref.shape[0]
    span = 2 * length
    group = GROUP * length
    scale = HDIM**-0.5
    tiles = packs_ref[...].astype(f32)
    own_ranks = tiles[RANK_ROW : RANK_ROW + 1]
    far_ranks = tiles[PACK + RANK_ROW : PACK + RANK_ROW + 1]
    ranks = jnp.concatenate([own_ranks, far_ranks], 1)
    move = (iota((span, span), 0).astype(f32) == ranks).astype(f32)
    home_ref[...] = jnp.transpose(move).astype(bf16)
    in_order = jnp.dot(
        move.astype(bf16), jnp.concatenate([kv_ref[...], far_ref[...]], 0), preferred_element_type=f32
    ).astype(bf16)
    column = jnp.transpose(jnp.broadcast_to(own_ranks, (length, length)))
    first = (column < BUCKET).astype(f32)
    first_ref[...] = first
    for j in range(KV_HEADS):
        at = slice(j * group, (j + 1) * group)
        keys = jnp.concatenate([in_order[:BUCKET, columns(j)], in_order[BUCKET:, columns(j)]], 1)
        keys2_ref[:, 2 * j * HDIM : 2 * (j + 1) * HDIM] = keys
        to = columns(KV_HEADS + j)
        values = jnp.concatenate([in_order[:BUCKET, to], in_order[BUCKET:, to]], 1)
        query = by_bucket(stacked(query_ref, j), first)
        grad = by_bucket(stacked(grad_ref, j), first)
        score = lax.dot_general(keys, query, NT, preferred_element_type=f32) * scale
        heads = range(j * GROUP, (j + 1) * GROUP)
        sink = jnp.concatenate([jnp.broadcast_to(sink_ref[:, h : h + 1], (1, length)) for h in heads], 1)
        top = jnp.maximum(jnp.max(score, axis=0, keepdims=True), sink)
        weight = jnp.exp(score - top)
        sink_weight = jnp.exp(sink - top)
        weight_ref[:, at] = weight
        up = lax.dot_general(values, grad, NT, preferred_element_type=f32)
        up_ref[:, at] = up
        stats_ref[0:1, at] = top
        stats_ref[1:2, at] = jnp.sum(weight, axis=0, keepdims=True) + sink_weight
        stats_ref[2:3, at] = jnp.sum(weight * up, axis=0, keepdims=True)
        stats_ref[3:4, at] = sink_weight


def terms_kernel(
    slots, query_ref, grad_ref, weight_ref, up_ref, stats_ref, packs_ref,
    out_hbm, ds_ref, half_ref, slot_keys_ref, out_ref, rows_ref, sinks_ref, tiles_ref, sem,
):
    length = query_ref.shape[1]
    group = GROUP * length
    padded = -(-slots // 16) * 16
    order = slot_order(slots)
    scale = HDIM**-0.5
    tiles_ref[...] = packs_ref[...].astype(f32)

    def chosen(row):
        part = tiles_ref[pl.ds(row, slots, stride=PACK), :]
        if padded > slots:
            part = jnp.concatenate([part, jnp.zeros((padded - slots, HDIM), f32)], 0)
        return part

    slot_keys = [chosen(j).astype(bf16) for j in range(KV_HEADS)]
    slot_values = [chosen(KV_HEADS + j).astype(bf16) for j in range(KV_HEADS)]
    slot_keys_ref[...] = jnp.concatenate(slot_keys, 1)
    own_marks = (tiles_ref[RANK_ROW : RANK_ROW + 1] >= BUCKET).astype(f32)
    slot_at = iota((padded, length), 0)
    bias = jnp.log(jnp.maximum(chosen(COUNT_ROW), 1.0))
    same = (slot_at < 2) & (chosen(MARK_ROW) == own_marks)
    bias = jnp.where(same | (slot_at >= slots), NEG, bias)
    query = [stacked(query_ref, j) for j in range(KV_HEADS)]
    grad = [stacked(grad_ref, j) for j in range(KV_HEADS)]

    def against(parts, rows):
        return jnp.concatenate(
            [lax.dot_general(part, row, NT, preferred_element_type=f32) for part, row in zip(parts, rows)], 1
        )

    score = against(slot_keys, query) * scale + jnp.concatenate([bias] * HEADS, 1)
    up = against(slot_values, grad)
    pair_top = stats_ref[0:1]
    top = jnp.maximum(pair_top, jnp.max(score, axis=0, keepdims=True))
    weight = jnp.exp(score - top)
    pair_scale = jnp.exp(pair_top - top)
    inverse = 1.0 / (pair_scale * stats_ref[1:2] + jnp.sum(weight, axis=0, keepdims=True))
    pair_scale = pair_scale * inverse
    prob = weight * inverse
    delta = pair_scale * stats_ref[2:3] + jnp.sum(prob * up, axis=0, keepdims=True)
    ds = (prob * (up - delta)).astype(bf16)
    half = prob.astype(bf16)
    ds_ref[length:] = ds
    rows_ref[0:1] = pair_scale
    rows_ref[1:2] = delta
    sink_rows = pair_scale * stats_ref[3:4] * delta
    for h in range(HEADS):
        sinks_ref[h : h + 1] = sink_rows[:, h * length : (h + 1) * length]
    sinks = jnp.sum(sinks_ref[...], axis=1, keepdims=True)
    sinks = jnp.where(iota((HEADS, HDIM), 0) == iota((HEADS, HDIM), 1), -sinks, 0.0)
    sinks = jnp.sum(sinks, axis=0, keepdims=True)
    high = sinks.astype(bf16).astype(f32)
    ends = (high, sinks - high)

    def piece(first, second):
        shape = out_ref.shape[1:]
        upper = jnp.broadcast_to(jnp.concatenate([first, ends[0]], 1), shape)
        lower = jnp.broadcast_to(jnp.concatenate([second, ends[1]], 1), shape)
        return jnp.where(iota(shape, 0) == 0, upper, lower).astype(bf16)

    nothing = jnp.zeros((1, KV_HEADS * HDIM), f32)
    out_ref[...] = jnp.broadcast_to(piece(nothing, nothing)[None], out_ref.shape)
    key_rows, value_rows = (
        jnp.concatenate(
            [
                lax.dot_general(left[:, j * group : (j + 1) * group], right[j], NN, preferred_element_type=f32)
                for j in range(KV_HEADS)
            ],
            1,
        )
        for left, right in ((ds, query), (half, grad))
    )
    key_rows = key_rows * scale
    first = lax.axis_index("dp") * slots
    for slot in range(slots):
        out_ref[first + (lax.axis_index("ctx") ^ order[slot])] = piece(
            key_rows[slot : slot + 1], value_rows[slot : slot + 1]
        )
    copy = pltpu.make_async_copy(out_ref, out_hbm, sem)
    copy.start()

    @pl.loop(0, KV_HEADS)
    def _(j):
        at = pl.ds(pl.multiple_of(j * group, group), group)
        pair_prob = weight_ref[:, at] * rows_ref[0:1, at]
        ds_ref[pl.ds(0, length), at] = (pair_prob * (up_ref[:, at] - rows_ref[1:2, at])).astype(bf16)
        half_ref[:, at] = pair_prob.astype(bf16)

    copy.wait()


def gradient_kernel(
    query_ref, grad_ref, ds_ref, half_ref, slot_keys_ref, keys2_ref, home_ref, first_ref,
    dq_hbm, own_grad_ref, *refs,
):
    far_grad_refs, (dq_ref, sems) = refs[:-2], refs[-2:]
    length = first_ref.shape[0]
    group = GROUP * length
    wide = KV_HEADS * HDIM
    scale = HDIM**-0.5
    mine = jnp.concatenate([first_ref[...]] * GROUP, 0) > 0.5
    sent = []
    grads = [[], []]
    for j in range(KV_HEADS):
        at = slice(j * group, (j + 1) * group)
        slot_keys = slot_keys_ref[:, columns(j)]
        keys = jnp.concatenate(
            [keys2_ref[:, 2 * j * HDIM : 2 * (j + 1) * HDIM], jnp.concatenate([slot_keys, slot_keys], 1)], 0
        )
        dq = lax.dot_general(ds_ref[:, at], keys, TN, preferred_element_type=f32)
        dq = (jnp.where(mine, dq[:, :HDIM], dq[:, HDIM:]) * scale).astype(bf16)
        for g in range(GROUP):
            dq_ref[:, columns(j * GROUP + g)] = dq[g * length : (g + 1) * length]
        to = pl.ds(j * GROUP * HDIM, GROUP * HDIM)
        copy = pltpu.make_async_copy(dq_ref.at[:, to], dq_hbm.at[0, :, to], sems.at[j])
        copy.start()
        sent.append(copy)
        query = by_bucket(stacked(query_ref, j), first_ref[...])
        grad = by_bucket(stacked(grad_ref, j), first_ref[...])
        dk = lax.dot_general(ds_ref[:length, at], query, NN, preferred_element_type=f32) * scale
        dv = lax.dot_general(half_ref[:, at], grad, NN, preferred_element_type=f32)
        for i, part in enumerate((dk, dv)):
            grads[i].append(jnp.concatenate([part[:, :HDIM], part[:, HDIM:]], 0).astype(bf16))
    for i in range(2):
        at = slice(i * wide, (i + 1) * wide)
        back = jnp.dot(home_ref[...], jnp.concatenate(grads[i], 1), preferred_element_type=f32)
        own_grad_ref[:, at] = back[:length]
        for part in range(1):
            far_grad_refs[i * 1 + part][...] = back[length:, part * 512 : (part + 1) * 512].astype(bf16)
    for copy in sent:
        copy.wait()


def last_kernel(slots, meta_ref, own_ref, terms_ref, *refs):
    recv_refs, (dk_ref, dv_ref, sink_ref) = refs[:-3], refs[-3:]
    length = own_ref.shape[0]
    wide = KV_HEADS * HDIM
    ends = jnp.sum(terms_ref[:, :, wide:].astype(f32), axis=0)
    sink_ref[...] = (ends[0:1] + ends[1:2])[:, :HEADS]
    first = lax.axis_index("dp") * slots
    slot = jnp.sum(terms_ref[pl.ds(first, slots), :, :wide].astype(f32), axis=0)
    mine = iota((length, HDIM), 0).astype(f32) == meta_ref[0:1]
    for i, out_ref in enumerate((dk_ref, dv_ref)):
        for j in range(KV_HEADS):
            at = columns(i * KV_HEADS + j)
            total = own_ref[:, at] + recv_refs[(i * KV_HEADS + j) * HDIM // 512][:, columns((i * KV_HEADS + j) % 4)].astype(f32)
            total = total + jnp.where(mine, slot[i : i + 1, columns(j)], 0.0)
            out_ref[0, :, columns(j)] = total.astype(bf16)


def on_device(
    query_rows, key_rows, value_rows, grad_rows, bucket_rank, sample_rows, sample_count, sink_logit
):
    length = query_rows.shape[1]
    wide = KV_HEADS * HDIM
    slots = lax.axis_size("ctx")
    rows = HEADS * HDIM
    token = pl.pallas_call(
        token_kernel,
        out_shape=jax.ShapeDtypeStruct((PACK, length), jnp.int32),
        out_specs=VMEM,
        compiler_params=SMALL,
        cost_estimate=LOADS,
        name="token_lanes",
    )()
    sample_rows, sample_count, token = lax.optimization_barrier((sample_rows, sample_count, token))
    kv, tile, meta = pl.pallas_call(
        pack_kernel,
        out_shape=[
            jax.ShapeDtypeStruct((length, 2 * wide), bf16),
            jax.ShapeDtypeStruct((PACK, HDIM), bf16),
            jax.ShapeDtypeStruct((8, length), f32),
        ],
        in_specs=[SMEM] * 2 + [VMEM] * 4,
        out_specs=[VMEM] * 3,
        compiler_params=SMALL,
        cost_estimate=LOADS,
        name="pack_sample",
    )(sample_rows, sample_count, token, bucket_rank, key_rows, value_rows)

    far_tile = moved(tile, "ctx", 1)
    far_kv = moved(kv, "ctx", 1)
    packs = jnp.concatenate([tile, far_tile], 0)
    by_token = jax.ShapeDtypeStruct((length, rows), f32)
    weight, up, stats, keys2, home, first, same = pl.pallas_call(
        score_kernel,
        out_shape=[
            by_token,
            by_token,
            jax.ShapeDtypeStruct((8, rows), f32),
            jax.ShapeDtypeStruct((length, 2 * wide), bf16),
            jax.ShapeDtypeStruct((2 * length, 2 * length), bf16),
            jax.ShapeDtypeStruct((length, length), f32),
            jax.ShapeDtypeStruct(packs.shape, bf16),
        ],
        in_specs=[VMEM] * 6,
        out_specs=[VMEM] * 7,
        compiler_params=LARGE,
        cost_estimate=pl.CostEstimate(
            flops=8 * length * length * rows, transcendentals=2 * length * rows, bytes_accessed=20 * length * rows
        ),
        name="pair_scores",
    )(query_rows, grad_rows, kv, far_kv, packs, sink_logit[None])
    for offsets in rounds(slots):
        arrived = [moved(packs, "ctx", d) for d in offsets]
        packs = jnp.concatenate([same] + arrived, 0)
        same = packs
    devices = slots * lax.axis_size("dp")
    padded = -(-slots // 16) * 16
    terms, ds, half, slot_keys = pl.pallas_call(
        functools.partial(terms_kernel, slots),
        out_shape=[
            jax.ShapeDtypeStruct((devices, 2, wide + HDIM), bf16),
            jax.ShapeDtypeStruct((length + padded, rows), bf16),
            jax.ShapeDtypeStruct((length, rows), bf16),
            jax.ShapeDtypeStruct((padded, wide), bf16),
        ],
        in_specs=[VMEM] * 6,
        out_specs=[HBM] + [VMEM] * 3,
        scratch_shapes=[
            pltpu.VMEM((devices, 2, wide + HDIM), bf16),
            pltpu.VMEM((8, rows), f32),
            pltpu.VMEM((HEADS, length), f32),
            pltpu.VMEM((slots * PACK, HDIM), f32),
            pltpu.SemaphoreType.DMA,
        ],
        compiler_params=LARGE,
        name="slot_terms",
    )(query_rows, grad_rows, weight, up, stats, packs)
    terms = lax.all_to_all(terms, ("dp", "ctx"), 0, 0, tiled=True)
    dq, own, *far = pl.pallas_call(
        gradient_kernel,
        out_shape=[
            jax.ShapeDtypeStruct((1, length, rows), bf16),
            jax.ShapeDtypeStruct((length, 2 * wide), f32),
        ]
        + [jax.ShapeDtypeStruct((length, 2 * wide // 2), bf16)] * 2,
        in_specs=[VMEM] * 8,
        out_specs=[HBM] + [VMEM] * 3,
        scratch_shapes=[pltpu.VMEM((length, rows), bf16), pltpu.SemaphoreType.DMA((KV_HEADS,))],
        compiler_params=LARGE,
        cost_estimate=pl.CostEstimate(
            flops=12 * length * length * rows, transcendentals=0, bytes_accessed=20 * length * rows
        ),
        name="gradients",
    )(query_rows, grad_rows, ds, half, slot_keys, keys2, home, first)
    recv = [moved(part, "ctx", 1) for part in far]
    dk, dv, sink_grad = pl.pallas_call(
        functools.partial(last_kernel, slots),
        out_shape=[jax.ShapeDtypeStruct((1, length, wide), bf16)] * 2
        + [jax.ShapeDtypeStruct((1, HEADS), f32)],
        in_specs=[VMEM] * 5,
        out_specs=[VMEM] * 3,
        compiler_params=SMALL,
        name="add_up",
    )(meta, own, terms, *recv)
    return dq, dk, dv, sink_grad[0]


def solution(mesh):
    return jax.shard_map(
        on_device,
        mesh=mesh,
        in_specs=(
            P("dp", "ctx", None),
            P("dp", "ctx", None),
            P("dp", "ctx", None),
            P("dp", "ctx", None),
            P("dp", "ctx"),
            P("dp", "ctx"),
            P("dp", "ctx"),
            P(),
        ),
        out_specs=(P("dp", "ctx", None), P("dp", "ctx", None), P("dp", "ctx", None), P()),
        check_vma=False,
    )
```

```python
import functools

import jax
import jax.numpy as jnp
from jax import lax
from jax.experimental import pallas as pl
from jax.experimental.pallas import tpu as pltpu
from jax.sharding import PartitionSpec as P

HEADS = 16
KV_HEADS = 4
HDIM = 128
BUCKET = 128
GROUP = HEADS // KV_HEADS
NEG = -1e30
PACK = 16
COUNT_ROW = 8
MARK_ROW = 9
RANK_ROW = 10

f32 = jnp.float32
bf16 = jnp.bfloat16
NN = (((1,), (0,)), ((), ()))
NT = (((1,), (1,)), ((), ()))
TN = (((0,), (0,)), ((), ()))
VMEM = pl.BlockSpec(memory_space=pltpu.VMEM)
SMEM = pl.BlockSpec(memory_space=pltpu.SMEM)
HBM = pl.BlockSpec(memory_space=pltpu.HBM)
LARGE = pltpu.CompilerParams(vmem_limit_bytes=24 * 1024 * 1024)
LOADS = pl.CostEstimate(flops=10**10, transcendentals=0, bytes_accessed=10**7)
SMALL = pltpu.CompilerParams(vmem_limit_bytes=6 * 1024 * 1024)


def in_hbm(*arrays):
    return [pltpu.with_memory_space_constraint(array, pltpu.HBM) for array in arrays]


def moved(array, axis, apart):
    return lax.ppermute(array, axis, [(i, i ^ apart) for i in range(lax.axis_size(axis))])


def rounds(size):
    found, base = [], 2
    while base < size:
        found.append([base + 1] if base * 2 >= size else [base + 1, 2 * base + 1, 3 * base + 1])
        base *= 2 if base * 2 >= size else 4
    return found


def slot_order(size):
    order = [0, 1]
    for offsets in rounds(size):
        order = order + [d ^ near for d in offsets for near in order]
    return order


def iota(shape, dim):
    return lax.broadcasted_iota(jnp.int32, shape, dim)


def token_kernel(out_ref):
    out_ref[...] = iota(out_ref.shape, 1)


def pack_kernel(
    row_ref, count_ref, token_ref, rank_ref, keys_ref, values_ref, kv_ref, out_ref, meta_ref
):
    wide = keys_ref.shape[2]
    kv_ref[:, :wide] = keys_ref[0]
    kv_ref[:, wide:] = values_ref[0]
    length = kv_ref.shape[0]
    row = row_ref[0, 0]
    pick = (token_ref[...] == row).astype(bf16)
    picked = jnp.dot(pick, kv_ref[...], preferred_element_type=f32)
    ranks = rank_ref[...].astype(f32)
    mark = jnp.sum(jnp.where(token_ref[:1] == row, ranks, 0.0), axis=1, keepdims=True)
    mark = (mark >= BUCKET).astype(f32)
    at = iota((PACK, HDIM), 0)
    tile = jnp.zeros((PACK, HDIM), f32)
    for j in range(2 * KV_HEADS):
        tile = jnp.where(at == j, picked[:, j * HDIM : (j + 1) * HDIM], tile)
    tile = jnp.where(at == COUNT_ROW, count_ref[0, 0].astype(f32), tile)
    tile = jnp.where(at == MARK_ROW, mark, tile)
    tile = jnp.where(at == RANK_ROW, ranks, tile)
    out_ref[...] = tile.astype(bf16)
    at = iota((8, length), 0)
    meta = jnp.where(at == 0, row.astype(f32), 0.0)
    meta_ref[...] = meta


def columns(j):
    return slice(j * HDIM, (j + 1) * HDIM)


def stacked(ref, j):
    return jnp.concatenate([ref[0, :, columns(j * GROUP + g)] for g in range(GROUP)], 0)


def by_bucket(rows, first):
    low = jnp.concatenate([first] * GROUP, 0).astype(bf16)
    high = jnp.concatenate([1.0 - first] * GROUP, 0).astype(bf16)
    return jnp.concatenate([rows * low, rows * high], 1)


def score_kernel(
    query_ref, grad_ref, kv_ref, far_ref, packs_ref, sink_ref,
    weight_ref, up_ref, stats_ref, keys2_ref, home_ref, first_ref, same_ref,
):
    same_ref[...] = packs_ref[...]
    length = kv_ref.shape[0]
    span = 2 * length
    group = GROUP * length
    scale = HDIM**-0.5
    tiles = packs_ref[...].astype(f32)
    own_ranks = tiles[RANK_ROW : RANK_ROW + 1]
    far_ranks = tiles[PACK + RANK_ROW : PACK + RANK_ROW + 1]
    ranks = jnp.concatenate([own_ranks, far_ranks], 1)
    move = (iota((span, span), 0).astype(f32) == ranks).astype(f32)
    home_ref[...] = jnp.transpose(move).astype(bf16)
    in_order = jnp.dot(
        move.astype(bf16), jnp.concatenate([kv_ref[...], far_ref[...]], 0), preferred_element_type=f32
    ).astype(bf16)
    column = jnp.transpose(jnp.broadcast_to(own_ranks, (length, length)))
    first = (column < BUCKET).astype(f32)
    first_ref[...] = first
    for j in range(KV_HEADS):
        at = slice(j * group, (j + 1) * group)
        keys = jnp.concatenate([in_order[:BUCKET, columns(j)], in_order[BUCKET:, columns(j)]], 1)
        keys2_ref[:, 2 * j * HDIM : 2 * (j + 1) * HDIM] = keys
        to = columns(KV_HEADS + j)
        values = jnp.concatenate([in_order[:BUCKET, to], in_order[BUCKET:, to]], 1)
        query = by_bucket(stacked(query_ref, j), first)
        grad = by_bucket(stacked(grad_ref, j), first)
        score = lax.dot_general(keys, query, NT, preferred_element_type=f32) * scale
        heads = range(j * GROUP, (j + 1) * GROUP)
        sink = jnp.concatenate([jnp.broadcast_to(sink_ref[:, h : h + 1], (1, length)) for h in heads], 1)
        top = jnp.maximum(jnp.max(score, axis=0, keepdims=True), sink)
        weight = jnp.exp(score - top)
        sink_weight = jnp.exp(sink - top)
        weight_ref[:, at] = weight
        up = lax.dot_general(values, grad, NT, preferred_element_type=f32)
        up_ref[:, at] = up
        stats_ref[0:1, at] = top
        stats_ref[1:2, at] = jnp.sum(weight, axis=0, keepdims=True) + sink_weight
        stats_ref[2:3, at] = jnp.sum(weight * up, axis=0, keepdims=True)
        stats_ref[3:4, at] = sink_weight


def terms_kernel(
    slots, query_ref, grad_ref, weight_ref, up_ref, stats_ref, packs_ref,
    out_hbm, ds_ref, half_ref, slot_keys_ref, out_ref, rows_ref, sinks_ref, tiles_ref, sem,
):
    length = query_ref.shape[1]
    group = GROUP * length
    padded = -(-slots // 16) * 16
    order = slot_order(slots)
    scale = HDIM**-0.5
    tiles_ref[...] = packs_ref[...].astype(f32)

    def chosen(row):
        part = tiles_ref[pl.ds(row, slots, stride=PACK), :]
        if padded > slots:
            part = jnp.concatenate([part, jnp.zeros((padded - slots, HDIM), f32)], 0)
        return part

    slot_keys = [chosen(j).astype(bf16) for j in range(KV_HEADS)]
    slot_values = [chosen(KV_HEADS + j).astype(bf16) for j in range(KV_HEADS)]
    slot_keys_ref[...] = jnp.concatenate(slot_keys, 1)
    own_marks = (tiles_ref[RANK_ROW : RANK_ROW + 1] >= BUCKET).astype(f32)
    slot_at = iota((padded, length), 0)
    bias = jnp.log(jnp.maximum(chosen(COUNT_ROW), 1.0))
    same = (slot_at < 2) & (chosen(MARK_ROW) == own_marks)
    bias = jnp.where(same | (slot_at >= slots), NEG, bias)
    query = [stacked(query_ref, j) for j in range(KV_HEADS)]
    grad = [stacked(grad_ref, j) for j in range(KV_HEADS)]

    def against(parts, rows):
        return jnp.concatenate(
            [lax.dot_general(part, row, NT, preferred_element_type=f32) for part, row in zip(parts, rows)], 1
        )

    score = against(slot_keys, query) * scale + jnp.concatenate([bias] * HEADS, 1)
    up = against(slot_values, grad)
    pair_top = stats_ref[0:1]
    top = jnp.maximum(pair_top, jnp.max(score, axis=0, keepdims=True))
    weight = jnp.exp(score - top)
    pair_scale = jnp.exp(pair_top - top)
    inverse = 1.0 / (pair_scale * stats_ref[1:2] + jnp.sum(weight, axis=0, keepdims=True))
    pair_scale = pair_scale * inverse
    prob = weight * inverse
    delta = pair_scale * stats_ref[2:3] + jnp.sum(prob * up, axis=0, keepdims=True)
    ds = (prob * (up - delta)).astype(bf16)
    half = prob.astype(bf16)
    ds_ref[length:] = ds
    rows_ref[0:1] = pair_scale
    rows_ref[1:2] = delta
    sink_rows = pair_scale * stats_ref[3:4] * delta
    for h in range(HEADS):
        sinks_ref[h : h + 1] = sink_rows[:, h * length : (h + 1) * length]
    sinks = jnp.sum(sinks_ref[...], axis=1, keepdims=True)
    sinks = jnp.where(iota((HEADS, HDIM), 0) == iota((HEADS, HDIM), 1), -sinks, 0.0)
    sinks = jnp.sum(sinks, axis=0, keepdims=True)
    high = sinks.astype(bf16).astype(f32)
    ends = (high, sinks - high)

    def piece(first, second):
        shape = out_ref.shape[1:]
        upper = jnp.broadcast_to(jnp.concatenate([first, ends[0]], 1), shape)
        lower = jnp.broadcast_to(jnp.concatenate([second, ends[1]], 1), shape)
        return jnp.where(iota(shape, 0) == 0, upper, lower).astype(bf16)

    nothing = jnp.zeros((1, KV_HEADS * HDIM), f32)
    out_ref[...] = jnp.broadcast_to(piece(nothing, nothing)[None], out_ref.shape)
    key_rows, value_rows = (
        jnp.concatenate(
            [
                lax.dot_general(left[:, j * group : (j + 1) * group], right[j], NN, preferred_element_type=f32)
                for j in range(KV_HEADS)
            ],
            1,
        )
        for left, right in ((ds, query), (half, grad))
    )
    key_rows = key_rows * scale
    first = lax.axis_index("dp") * slots
    for slot in range(slots):
        out_ref[first + (lax.axis_index("ctx") ^ order[slot])] = piece(
            key_rows[slot : slot + 1], value_rows[slot : slot + 1]
        )
    copy = pltpu.make_async_copy(out_ref, out_hbm, sem)
    copy.start()

    @pl.loop(0, KV_HEADS)
    def _(j):
        at = pl.ds(pl.multiple_of(j * group, group), group)
        pair_prob = weight_ref[:, at] * rows_ref[0:1, at]
        ds_ref[pl.ds(0, length), at] = (pair_prob * (up_ref[:, at] - rows_ref[1:2, at])).astype(bf16)
        half_ref[:, at] = pair_prob.astype(bf16)

    copy.wait()


def gradient_kernel(
    query_ref, grad_ref, ds_ref, half_ref, slot_keys_ref, keys2_ref, home_ref, first_ref,
    dq_hbm, own_grad_ref, *refs,
):
    far_grad_refs, (dq_ref, sems) = refs[:-2], refs[-2:]
    length = first_ref.shape[0]
    group = GROUP * length
    wide = KV_HEADS * HDIM
    scale = HDIM**-0.5
    mine = jnp.concatenate([first_ref[...]] * GROUP, 0) > 0.5
    sent = []
    grads = [[], []]
    for j in range(KV_HEADS):
        at = slice(j * group, (j + 1) * group)
        slot_keys = slot_keys_ref[:, columns(j)]
        keys = jnp.concatenate(
            [keys2_ref[:, 2 * j * HDIM : 2 * (j + 1) * HDIM], jnp.concatenate([slot_keys, slot_keys], 1)], 0
        )
        dq = lax.dot_general(ds_ref[:, at], keys, TN, preferred_element_type=f32)
        dq = (jnp.where(mine, dq[:, :HDIM], dq[:, HDIM:]) * scale).astype(bf16)
        for g in range(GROUP):
            dq_ref[:, columns(j * GROUP + g)] = dq[g * length : (g + 1) * length]
        to = pl.ds(j * GROUP * HDIM, GROUP * HDIM)
        copy = pltpu.make_async_copy(dq_ref.at[:, to], dq_hbm.at[0, :, to], sems.at[j])
        copy.start()
        sent.append(copy)
        query = by_bucket(stacked(query_ref, j), first_ref[...])
        grad = by_bucket(stacked(grad_ref, j), first_ref[...])
        dk = lax.dot_general(ds_ref[:length, at], query, NN, preferred_element_type=f32) * scale
        dv = lax.dot_general(half_ref[:, at], grad, NN, preferred_element_type=f32)
        for i, part in enumerate((dk, dv)):
            grads[i].append(jnp.concatenate([part[:, :HDIM], part[:, HDIM:]], 0))
    for i in range(2):
        in_order = jnp.concatenate(grads[i], 1)
        high = in_order.astype(bf16)
        low = (in_order - high.astype(f32)).astype(bf16)
        back = jnp.dot(home_ref[...], high, preferred_element_type=f32)
        rest = jnp.dot(home_ref[:length], low, preferred_element_type=f32)
        own_grad_ref[:, i * wide : (i + 1) * wide] = back[:length] + rest
        far_grad_refs[i][...] = back[length:].astype(bf16)
    for copy in sent:
        copy.wait()


def total_kernel(meta_ref, own_ref, key_recv_ref, value_recv_ref, total_ref, row_ref):
    length = own_ref.shape[0]
    mine = iota((length, HDIM), 0).astype(f32) == meta_ref[0:1]
    for i, recv_ref in enumerate((key_recv_ref, value_recv_ref)):
        for j in range(KV_HEADS):
            at = columns(i * KV_HEADS + j)
            total = own_ref[:, at] + recv_ref[:, columns(j)].astype(f32)
            total_ref[:, at] = total.astype(bf16)
            row = jnp.sum(jnp.where(mine, total, 0.0), axis=0, keepdims=True)
            row_ref[i : i + 1, columns(j)] = row


def last_kernel(slots, meta_ref, total_ref, row_ref, terms_ref, dk_ref, dv_ref, sink_ref):
    length = total_ref.shape[0]
    wide = KV_HEADS * HDIM
    ends = jnp.sum(terms_ref[:, :, wide:].astype(f32), axis=0)
    sink_ref[...] = (ends[0:1] + ends[1:2])[:, :HEADS]
    first = lax.axis_index("dp") * slots
    row = row_ref[0:2] + jnp.sum(terms_ref[pl.ds(first, slots), :, :wide].astype(f32), axis=0)
    mine = iota((length, HDIM), 0).astype(f32) == meta_ref[0:1]
    for i, out_ref in enumerate((dk_ref, dv_ref)):
        for j in range(KV_HEADS):
            total = total_ref[:, columns(i * KV_HEADS + j)].astype(f32)
            out_ref[0, :, columns(j)] = jnp.where(mine, row[i : i + 1, columns(j)], total).astype(bf16)


def on_device(
    query_rows, key_rows, value_rows, grad_rows, bucket_rank, sample_rows, sample_count, sink_logit
):
    length = query_rows.shape[1]
    wide = KV_HEADS * HDIM
    slots = lax.axis_size("ctx")
    rows = HEADS * HDIM
    token = pl.pallas_call(
        token_kernel,
        out_shape=jax.ShapeDtypeStruct((PACK, length), jnp.int32),
        out_specs=VMEM,
        compiler_params=SMALL,
        cost_estimate=LOADS,
        name="token_lanes",
    )()
    sample_rows, sample_count, token = lax.optimization_barrier((sample_rows, sample_count, token))
    kv, tile, meta = pl.pallas_call(
        pack_kernel,
        out_shape=[
            jax.ShapeDtypeStruct((length, 2 * wide), bf16),
            jax.ShapeDtypeStruct((PACK, HDIM), bf16),
            jax.ShapeDtypeStruct((8, length), f32),
        ],
        in_specs=[SMEM] * 2 + [VMEM] * 4,
        out_specs=[VMEM] * 3,
        compiler_params=SMALL,
        cost_estimate=LOADS,
        name="pack_sample",
    )(sample_rows, sample_count, token, bucket_rank, key_rows, value_rows)

    far_tile = moved(tile, "ctx", 1)
    far_kv = moved(kv, "ctx", 1)
    packs = jnp.concatenate([tile, far_tile], 0)
    by_token = jax.ShapeDtypeStruct((length, rows), f32)
    weight, up, stats, keys2, home, first, same = pl.pallas_call(
        score_kernel,
        out_shape=[
            by_token,
            by_token,
            jax.ShapeDtypeStruct((8, rows), f32),
            jax.ShapeDtypeStruct((length, 2 * wide), bf16),
            jax.ShapeDtypeStruct((2 * length, 2 * length), bf16),
            jax.ShapeDtypeStruct((length, length), f32),
            jax.ShapeDtypeStruct(packs.shape, bf16),
        ],
        in_specs=[VMEM] * 6,
        out_specs=[VMEM] * 7,
        compiler_params=LARGE,
        cost_estimate=pl.CostEstimate(
            flops=8 * length * length * rows, transcendentals=2 * length * rows, bytes_accessed=20 * length * rows
        ),
        name="pair_scores",
    )(query_rows, grad_rows, kv, far_kv, packs, sink_logit[None])
    for offsets in rounds(slots):
        arrived = [moved(packs, "ctx", d) for d in offsets]
        packs = jnp.concatenate([same] + arrived, 0)
        same = packs
    devices = slots * lax.axis_size("dp")
    padded = -(-slots // 16) * 16
    terms, ds, half, slot_keys = pl.pallas_call(
        functools.partial(terms_kernel, slots),
        out_shape=[
            jax.ShapeDtypeStruct((devices, 2, wide + HDIM), bf16),
            jax.ShapeDtypeStruct((length + padded, rows), bf16),
            jax.ShapeDtypeStruct((length, rows), bf16),
            jax.ShapeDtypeStruct((padded, wide), bf16),
        ],
        in_specs=[VMEM] * 6,
        out_specs=[HBM] + [VMEM] * 3,
        scratch_shapes=[
            pltpu.VMEM((devices, 2, wide + HDIM), bf16),
            pltpu.VMEM((8, rows), f32),
            pltpu.VMEM((HEADS, length), f32),
            pltpu.VMEM((slots * PACK, HDIM), f32),
            pltpu.SemaphoreType.DMA,
        ],
        compiler_params=LARGE,
        name="slot_terms",
    )(query_rows, grad_rows, weight, up, stats, packs)
    terms = lax.all_to_all(terms, ("dp", "ctx"), 0, 0, tiled=True)
    dq, own, *far = pl.pallas_call(
        gradient_kernel,
        out_shape=[
            jax.ShapeDtypeStruct((1, length, rows), bf16),
            jax.ShapeDtypeStruct((length, 2 * wide), f32),
        ]
        + [jax.ShapeDtypeStruct((length, 2 * wide // 2), bf16)] * 2,
        in_specs=[VMEM] * 8,
        out_specs=[HBM] + [VMEM] * 3,
        scratch_shapes=[pltpu.VMEM((length, rows), bf16), pltpu.SemaphoreType.DMA((KV_HEADS,))],
        compiler_params=LARGE,
        cost_estimate=pl.CostEstimate(
            flops=12 * length * length * rows, transcendentals=0, bytes_accessed=20 * length * rows
        ),
        name="gradients",
    )(query_rows, grad_rows, ds, half, slot_keys, keys2, home, first)
    recv = [moved(part, "ctx", 1) for part in far]
    total, sampled = pl.pallas_call(
        total_kernel,
        out_shape=[
            jax.ShapeDtypeStruct((length, 2 * wide), bf16),
            jax.ShapeDtypeStruct((8, wide), f32),
        ],
        in_specs=[VMEM] * 4,
        out_specs=[VMEM] * 2,
        compiler_params=SMALL,
        name="pair_total",
    )(meta, own, *recv)
    dk, dv, sink_grad = pl.pallas_call(
        functools.partial(last_kernel, slots),
        out_shape=[jax.ShapeDtypeStruct((1, length, wide), bf16)] * 2
        + [jax.ShapeDtypeStruct((1, HEADS), f32)],
        in_specs=[VMEM] * 4,
        out_specs=[VMEM] * 3,
        compiler_params=SMALL,
        name="add_up",
    )(meta, total, sampled, terms)
    return dq, dk, dv, sink_grad[0]


def solution(mesh):
    return jax.shard_map(
        on_device,
        mesh=mesh,
        in_specs=(
            P("dp", "ctx", None),
            P("dp", "ctx", None),
            P("dp", "ctx", None),
            P("dp", "ctx", None),
            P("dp", "ctx"),
            P("dp", "ctx"),
            P("dp", "ctx"),
            P(),
        ),
        out_specs=(P("dp", "ctx", None), P("dp", "ctx", None), P("dp", "ctx", None), P()),
        check_vma=False,
    )
```

```python
import functools

import jax
import jax.numpy as jnp
from jax import lax
from jax.experimental import pallas as pl
from jax.experimental.pallas import tpu as pltpu
from jax.sharding import PartitionSpec as P

HEADS = 16
KV_HEADS = 4
HDIM = 128
BUCKET = 128
GROUP = HEADS // KV_HEADS
NEG = -1e30
PACK = 16
COUNT_ROW = 8
MARK_ROW = 9
RANK_ROW = 10

f32 = jnp.float32
bf16 = jnp.bfloat16
NN = (((1,), (0,)), ((), ()))
NT = (((1,), (1,)), ((), ()))
TN = (((0,), (0,)), ((), ()))
VMEM = pl.BlockSpec(memory_space=pltpu.VMEM)
SMEM = pl.BlockSpec(memory_space=pltpu.SMEM)
HBM = pl.BlockSpec(memory_space=pltpu.HBM)
LARGE = pltpu.CompilerParams(vmem_limit_bytes=24 * 1024 * 1024)
LOADS = pl.CostEstimate(flops=10**10, transcendentals=0, bytes_accessed=10**7)
SMALL = pltpu.CompilerParams(vmem_limit_bytes=6 * 1024 * 1024)


def in_hbm(*arrays):
    return [pltpu.with_memory_space_constraint(array, pltpu.HBM) for array in arrays]


def moved(array, axis, apart):
    return lax.ppermute(array, axis, [(i, i ^ apart) for i in range(lax.axis_size(axis))])


def rounds(size):
    found, base = [], 2
    while base < size:
        found.append([base + 1] if base * 2 >= size else [base + 1, 2 * base + 1, 3 * base + 1])
        base *= 2 if base * 2 >= size else 4
    return found


def slot_order(size):
    order = [0, 1]
    for offsets in rounds(size):
        order = order + [d ^ near for d in offsets for near in order]
    return order


def iota(shape, dim):
    return lax.broadcasted_iota(jnp.int32, shape, dim)


def token_kernel(out_ref):
    out_ref[...] = iota(out_ref.shape, 1)


def pack_kernel(
    row_ref, count_ref, token_ref, rank_ref, keys_ref, values_ref, kv_ref, out_ref, meta_ref
):
    wide = keys_ref.shape[2]
    kv_ref[:, :wide] = keys_ref[0]
    kv_ref[:, wide:] = values_ref[0]
    length = kv_ref.shape[0]
    row = row_ref[0, 0]
    pick = (token_ref[...] == row).astype(bf16)
    picked = jnp.dot(pick, kv_ref[...], preferred_element_type=f32)
    ranks = rank_ref[...].astype(f32)
    mark = jnp.sum(jnp.where(token_ref[:1] == row, ranks, 0.0), axis=1, keepdims=True)
    mark = (mark >= BUCKET).astype(f32)
    at = iota((PACK, HDIM), 0)
    tile = jnp.zeros((PACK, HDIM), f32)
    for j in range(2 * KV_HEADS):
        tile = jnp.where(at == j, picked[:, j * HDIM : (j + 1) * HDIM], tile)
    tile = jnp.where(at == COUNT_ROW, count_ref[0, 0].astype(f32), tile)
    tile = jnp.where(at == MARK_ROW, mark, tile)
    tile = jnp.where(at == RANK_ROW, ranks, tile)
    out_ref[...] = tile.astype(bf16)
    at = iota((8, length), 0)
    meta = jnp.where(at == 0, row.astype(f32), 0.0)
    meta_ref[...] = meta


def columns(j):
    return slice(j * HDIM, (j + 1) * HDIM)


def stacked(ref, j):
    return jnp.concatenate([ref[0, :, columns(j * GROUP + g)] for g in range(GROUP)], 0)


def by_bucket(rows, first):
    low = jnp.concatenate([first] * GROUP, 0).astype(bf16)
    high = jnp.concatenate([1.0 - first] * GROUP, 0).astype(bf16)
    return jnp.concatenate([rows * low, rows * high], 1)


def score_kernel(
    query_ref, grad_ref, kv_ref, far_ref, packs_ref, sink_ref,
    weight_ref, up_ref, stats_ref, keys2_ref, home_ref, first_ref, same_ref,
):
    same_ref[...] = packs_ref[...]
    length = kv_ref.shape[0]
    span = 2 * length
    group = GROUP * length
    scale = HDIM**-0.5
    tiles = packs_ref[...].astype(f32)
    own_ranks = tiles[RANK_ROW : RANK_ROW + 1]
    far_ranks = tiles[PACK + RANK_ROW : PACK + RANK_ROW + 1]
    ranks = jnp.concatenate([own_ranks, far_ranks], 1)
    move = (iota((span, span), 0).astype(f32) == ranks).astype(f32)
    home_ref[...] = jnp.transpose(move).astype(bf16)
    in_order = jnp.dot(
        move.astype(bf16), jnp.concatenate([kv_ref[...], far_ref[...]], 0), preferred_element_type=f32
    ).astype(bf16)
    column = jnp.transpose(jnp.broadcast_to(own_ranks, (length, length)))
    first = (column < BUCKET).astype(f32)
    first_ref[...] = first
    for j in range(KV_HEADS):
        at = slice(j * group, (j + 1) * group)
        keys = jnp.concatenate([in_order[:BUCKET, columns(j)], in_order[BUCKET:, columns(j)]], 1)
        keys2_ref[:, 2 * j * HDIM : 2 * (j + 1) * HDIM] = keys
        to = columns(KV_HEADS + j)
        values = jnp.concatenate([in_order[:BUCKET, to], in_order[BUCKET:, to]], 1)
        query = by_bucket(stacked(query_ref, j), first)
        grad = by_bucket(stacked(grad_ref, j), first)
        score = lax.dot_general(keys, query, NT, preferred_element_type=f32) * scale
        heads = range(j * GROUP, (j + 1) * GROUP)
        sink = jnp.concatenate([jnp.broadcast_to(sink_ref[:, h : h + 1], (1, length)) for h in heads], 1)
        top = jnp.maximum(jnp.max(score, axis=0, keepdims=True), sink)
        weight = jnp.exp(score - top)
        sink_weight = jnp.exp(sink - top)
        weight_ref[:, at] = weight
        up = lax.dot_general(values, grad, NT, preferred_element_type=f32)
        up_ref[:, at] = up
        stats_ref[0:1, at] = top
        stats_ref[1:2, at] = jnp.sum(weight, axis=0, keepdims=True) + sink_weight
        stats_ref[2:3, at] = jnp.sum(weight * up, axis=0, keepdims=True)
        stats_ref[3:4, at] = sink_weight


def terms_kernel(
    slots, query_ref, grad_ref, weight_ref, up_ref, stats_ref, packs_ref,
    out_hbm, ds_ref, half_ref, slot_keys_ref, out_ref, rows_ref, sinks_ref, tiles_ref, sem,
):
    length = query_ref.shape[1]
    group = GROUP * length
    padded = -(-slots // 16) * 16
    order = slot_order(slots)
    scale = HDIM**-0.5
    tiles_ref[...] = packs_ref[...].astype(f32)

    def chosen(row):
        part = tiles_ref[pl.ds(row, slots, stride=PACK), :]
        if padded > slots:
            part = jnp.concatenate([part, jnp.zeros((padded - slots, HDIM), f32)], 0)
        return part

    slot_keys = [chosen(j).astype(bf16) for j in range(KV_HEADS)]
    slot_values = [chosen(KV_HEADS + j).astype(bf16) for j in range(KV_HEADS)]
    slot_keys_ref[...] = jnp.concatenate(slot_keys, 1)
    own_marks = (tiles_ref[RANK_ROW : RANK_ROW + 1] >= BUCKET).astype(f32)
    slot_at = iota((padded, length), 0)
    bias = jnp.log(jnp.maximum(chosen(COUNT_ROW), 1.0))
    same = (slot_at < 2) & (chosen(MARK_ROW) == own_marks)
    bias = jnp.where(same | (slot_at >= slots), NEG, bias)
    query = [stacked(query_ref, j) for j in range(KV_HEADS)]
    grad = [stacked(grad_ref, j) for j in range(KV_HEADS)]

    def against(parts, rows):
        return jnp.concatenate(
            [lax.dot_general(part, row, NT, preferred_element_type=f32) for part, row in zip(parts, rows)], 1
        )

    score = against(slot_keys, query) * scale + jnp.concatenate([bias] * HEADS, 1)
    up = against(slot_values, grad)
    pair_top = stats_ref[0:1]
    top = jnp.maximum(pair_top, jnp.max(score, axis=0, keepdims=True))
    weight = jnp.exp(score - top)
    pair_scale = jnp.exp(pair_top - top)
    inverse = 1.0 / (pair_scale * stats_ref[1:2] + jnp.sum(weight, axis=0, keepdims=True))
    pair_scale = pair_scale * inverse
    prob = weight * inverse
    delta = pair_scale * stats_ref[2:3] + jnp.sum(prob * up, axis=0, keepdims=True)
    ds = (prob * (up - delta)).astype(bf16)
    half = prob.astype(bf16)
    ds_ref[length:] = ds
    rows_ref[0:1] = pair_scale
    rows_ref[1:2] = delta
    sink_rows = pair_scale * stats_ref[3:4] * delta
    for h in range(HEADS):
        sinks_ref[h : h + 1] = sink_rows[:, h * length : (h + 1) * length]
    sinks = jnp.sum(sinks_ref[...], axis=1, keepdims=True)
    sinks = jnp.where(iota((HEADS, HDIM), 0) == iota((HEADS, HDIM), 1), -sinks, 0.0)
    sinks = jnp.sum(sinks, axis=0, keepdims=True)
    high = sinks.astype(bf16).astype(f32)
    ends = (high, sinks - high)

    def piece(first, second):
        shape = out_ref.shape[1:]
        upper = jnp.broadcast_to(jnp.concatenate([first, ends[0]], 1), shape)
        lower = jnp.broadcast_to(jnp.concatenate([second, ends[1]], 1), shape)
        return jnp.where(iota(shape, 0) == 0, upper, lower).astype(bf16)

    nothing = jnp.zeros((1, KV_HEADS * HDIM), f32)
    out_ref[...] = jnp.broadcast_to(piece(nothing, nothing)[None], out_ref.shape)
    key_rows, value_rows = (
        jnp.concatenate(
            [
                lax.dot_general(left[:, j * group : (j + 1) * group], right[j], NN, preferred_element_type=f32)
                for j in range(KV_HEADS)
            ],
            1,
        )
        for left, right in ((ds, query), (half, grad))
    )
    key_rows = key_rows * scale
    first = lax.axis_index("dp") * slots
    for slot in range(slots):
        out_ref[first + (lax.axis_index("ctx") ^ order[slot])] = piece(
            key_rows[slot : slot + 1], value_rows[slot : slot + 1]
        )
    copy = pltpu.make_async_copy(out_ref, out_hbm, sem)
    copy.start()

    @pl.loop(0, KV_HEADS)
    def _(j):
        at = pl.ds(pl.multiple_of(j * group, group), group)
        pair_prob = weight_ref[:, at] * rows_ref[0:1, at]
        ds_ref[pl.ds(0, length), at] = (pair_prob * (up_ref[:, at] - rows_ref[1:2, at])).astype(bf16)
        half_ref[:, at] = pair_prob.astype(bf16)

    copy.wait()


def gradient_kernel(
    query_ref, grad_ref, ds_ref, half_ref, slot_keys_ref, keys2_ref, home_ref, first_ref,
    dq_hbm, own_grad_ref, *refs,
):
    far_grad_refs, (dq_ref, sems) = refs[:-2], refs[-2:]
    length = first_ref.shape[0]
    group = GROUP * length
    wide = KV_HEADS * HDIM
    scale = HDIM**-0.5
    mine = jnp.concatenate([first_ref[...]] * GROUP, 0) > 0.5
    sent = []
    grads = [[], []]
    for j in range(KV_HEADS):
        at = slice(j * group, (j + 1) * group)
        slot_keys = slot_keys_ref[:, columns(j)]
        keys = jnp.concatenate(
            [keys2_ref[:, 2 * j * HDIM : 2 * (j + 1) * HDIM], jnp.concatenate([slot_keys, slot_keys], 1)], 0
        )
        dq = lax.dot_general(ds_ref[:, at], keys, TN, preferred_element_type=f32)
        dq = (jnp.where(mine, dq[:, :HDIM], dq[:, HDIM:]) * scale).astype(bf16)
        for g in range(GROUP):
            dq_ref[:, columns(j * GROUP + g)] = dq[g * length : (g + 1) * length]
        to = pl.ds(j * GROUP * HDIM, GROUP * HDIM)
        copy = pltpu.make_async_copy(dq_ref.at[:, to], dq_hbm.at[0, :, to], sems.at[j])
        copy.start()
        sent.append(copy)
        query = by_bucket(stacked(query_ref, j), first_ref[...])
        grad = by_bucket(stacked(grad_ref, j), first_ref[...])
        dk = lax.dot_general(ds_ref[:length, at], query, NN, preferred_element_type=f32) * scale
        dv = lax.dot_general(half_ref[:, at], grad, NN, preferred_element_type=f32)
        for i, part in enumerate((dk, dv)):
            grads[i].append(jnp.concatenate([part[:, :HDIM], part[:, HDIM:]], 0))
    for i in range(2):
        in_order = jnp.concatenate(grads[i], 1)
        high = in_order.astype(bf16)
        low = (in_order - high.astype(f32)).astype(bf16)
        back = jnp.dot(home_ref[...], high, preferred_element_type=f32)
        rest = jnp.dot(home_ref[:length], low, preferred_element_type=f32)
        own_grad_ref[:, i * wide : (i + 1) * wide] = back[:length] + rest
        far_grad_refs[i][...] = back[length:].astype(bf16)
    for copy in sent:
        copy.wait()


def total_kernel(meta_ref, own_ref, key_recv_ref, value_recv_ref, dk_ref, dv_ref, block_ref):
    wide = KV_HEADS * HDIM
    row = jnp.max(meta_ref[0:1]).astype(jnp.int32)
    start = pl.multiple_of(row // PACK * PACK, PACK)
    for i, (recv_ref, out_ref) in enumerate(((key_recv_ref, dk_ref), (value_recv_ref, dv_ref))):
        for j in range(KV_HEADS):
            total = own_ref[:, columns(i * KV_HEADS + j)] + recv_ref[:, columns(j)].astype(f32)
            out_ref[0, :, columns(j)] = total.astype(bf16)
        at = slice(i * wide, (i + 1) * wide)
        block_ref[:, at] = own_ref[pl.ds(start, PACK), at] + recv_ref[pl.ds(start, PACK), :].astype(f32)


def last_kernel(
    slots, meta_ref, block_ref, terms_ref, dk_in, dv_in, dk_hbm, dv_hbm, sink_hbm, dk_ref, dv_ref, sink_ref, sems
):
    wide = KV_HEADS * HDIM
    row = jnp.max(meta_ref[0:1]).astype(jnp.int32)
    start = pl.multiple_of(row // PACK * PACK, PACK)
    first = lax.axis_index("dp") * slots
    terms = jnp.sum(terms_ref[pl.ds(first, slots), :, :wide].astype(f32), axis=0)
    mine = iota((PACK, wide), 0) == row - start
    sent = []
    for i, (out_ref, out_hbm) in enumerate(((dk_ref, dk_hbm), (dv_ref, dv_hbm))):
        block = block_ref[:, i * wide : (i + 1) * wide]
        out_ref[...] = (block + jnp.where(mine, terms[i : i + 1], 0.0)).astype(bf16)
        copy = pltpu.make_async_copy(out_ref, out_hbm.at[0, pl.ds(start, PACK), :], sems.at[i])
        copy.start()
        sent.append(copy)
    ends = jnp.sum(terms_ref[:, :, wide:].astype(f32), axis=0)
    sink_ref[...] = (ends[0:1] + ends[1:2])[:, :HEADS]
    copy = pltpu.make_async_copy(sink_ref, sink_hbm, sems.at[2])
    copy.start()
    sent.append(copy)
    for copy in sent:
        copy.wait()


def on_device(
    query_rows, key_rows, value_rows, grad_rows, bucket_rank, sample_rows, sample_count, sink_logit
):
    length = query_rows.shape[1]
    wide = KV_HEADS * HDIM
    slots = lax.axis_size("ctx")
    rows = HEADS * HDIM
    token = pl.pallas_call(
        token_kernel,
        out_shape=jax.ShapeDtypeStruct((PACK, length), jnp.int32),
        out_specs=VMEM,
        compiler_params=SMALL,
        cost_estimate=LOADS,
        name="token_lanes",
    )()
    sample_rows, sample_count, token = lax.optimization_barrier((sample_rows, sample_count, token))
    kv, tile, meta = pl.pallas_call(
        pack_kernel,
        out_shape=[
            jax.ShapeDtypeStruct((length, 2 * wide), bf16),
            jax.ShapeDtypeStruct((PACK, HDIM), bf16),
            jax.ShapeDtypeStruct((8, length), f32),
        ],
        in_specs=[SMEM] * 2 + [VMEM] * 4,
        out_specs=[VMEM] * 3,
        compiler_params=SMALL,
        cost_estimate=LOADS,
        name="pack_sample",
    )(sample_rows, sample_count, token, bucket_rank, key_rows, value_rows)

    far_tile = moved(tile, "ctx", 1)
    far_kv = moved(kv, "ctx", 1)
    packs = jnp.concatenate([tile, far_tile], 0)
    by_token = jax.ShapeDtypeStruct((length, rows), f32)
    weight, up, stats, keys2, home, first, same = pl.pallas_call(
        score_kernel,
        out_shape=[
            by_token,
            by_token,
            jax.ShapeDtypeStruct((8, rows), f32),
            jax.ShapeDtypeStruct((length, 2 * wide), bf16),
            jax.ShapeDtypeStruct((2 * length, 2 * length), bf16),
            jax.ShapeDtypeStruct((length, length), f32),
            jax.ShapeDtypeStruct(packs.shape, bf16),
        ],
        in_specs=[VMEM] * 6,
        out_specs=[VMEM] * 7,
        compiler_params=LARGE,
        cost_estimate=pl.CostEstimate(
            flops=8 * length * length * rows, transcendentals=2 * length * rows, bytes_accessed=20 * length * rows
        ),
        name="pair_scores",
    )(query_rows, grad_rows, kv, far_kv, packs, sink_logit[None])
    for offsets in rounds(slots):
        arrived = [moved(packs, "ctx", d) for d in offsets]
        packs = jnp.concatenate([same] + arrived, 0)
        same = packs
    devices = slots * lax.axis_size("dp")
    padded = -(-slots // 16) * 16
    terms, ds, half, slot_keys = pl.pallas_call(
        functools.partial(terms_kernel, slots),
        out_shape=[
            jax.ShapeDtypeStruct((devices, 2, wide + HDIM), bf16),
            jax.ShapeDtypeStruct((length + padded, rows), bf16),
            jax.ShapeDtypeStruct((length, rows), bf16),
            jax.ShapeDtypeStruct((padded, wide), bf16),
        ],
        in_specs=[VMEM] * 6,
        out_specs=[HBM] + [VMEM] * 3,
        scratch_shapes=[
            pltpu.VMEM((devices, 2, wide + HDIM), bf16),
            pltpu.VMEM((8, rows), f32),
            pltpu.VMEM((HEADS, length), f32),
            pltpu.VMEM((slots * PACK, HDIM), f32),
            pltpu.SemaphoreType.DMA,
        ],
        compiler_params=LARGE,
        name="slot_terms",
    )(query_rows, grad_rows, weight, up, stats, packs)
    terms = lax.all_to_all(terms, ("dp", "ctx"), 0, 0, tiled=True)
    dq, own, *far = pl.pallas_call(
        gradient_kernel,
        out_shape=[
            jax.ShapeDtypeStruct((1, length, rows), bf16),
            jax.ShapeDtypeStruct((length, 2 * wide), f32),
        ]
        + [jax.ShapeDtypeStruct((length, 2 * wide // 2), bf16)] * 2,
        in_specs=[VMEM] * 8,
        out_specs=[HBM] + [VMEM] * 3,
        scratch_shapes=[pltpu.VMEM((length, rows), bf16), pltpu.SemaphoreType.DMA((KV_HEADS,))],
        compiler_params=LARGE,
        cost_estimate=pl.CostEstimate(
            flops=12 * length * length * rows, transcendentals=0, bytes_accessed=20 * length * rows
        ),
        name="gradients",
    )(query_rows, grad_rows, ds, half, slot_keys, keys2, home, first)
    recv = [moved(part, "ctx", 1) for part in far]
    grad_shape = jax.ShapeDtypeStruct((1, length, wide), bf16)
    dk, dv, block = pl.pallas_call(
        total_kernel,
        out_shape=[grad_shape, grad_shape, jax.ShapeDtypeStruct((PACK, 2 * wide), f32)],
        in_specs=[VMEM] * 4,
        out_specs=[VMEM] * 3,
        compiler_params=SMALL,
        name="pair_total",
    )(meta, own, *recv)
    dk, dv, sink_grad = pl.pallas_call(
        functools.partial(last_kernel, slots),
        out_shape=[grad_shape, grad_shape, jax.ShapeDtypeStruct((1, HEADS), f32)],
        in_specs=[VMEM] * 3 + [HBM] * 2,
        out_specs=[HBM] * 3,
        scratch_shapes=[pltpu.VMEM((PACK, wide), bf16)] * 2
        + [pltpu.VMEM((1, HEADS), f32), pltpu.SemaphoreType.DMA((3,))],
        input_output_aliases={3: 0, 4: 1},
        compiler_params=SMALL,
        name="add_up",
    )(meta, block, terms, dk, dv)
    return dq, dk, dv, sink_grad[0]


def solution(mesh):
    return jax.shard_map(
        on_device,
        mesh=mesh,
        in_specs=(
            P("dp", "ctx", None),
            P("dp", "ctx", None),
            P("dp", "ctx", None),
            P("dp", "ctx", None),
            P("dp", "ctx"),
            P("dp", "ctx"),
            P("dp", "ctx"),
            P(),
        ),
        out_specs=(P("dp", "ctx", None), P("dp", "ctx", None), P("dp", "ctx", None), P()),
        check_vma=False,
    )
```

```python
import functools

import jax
import jax.numpy as jnp
from jax import lax
from jax.experimental import pallas as pl
from jax.experimental.pallas import tpu as pltpu
from jax.sharding import PartitionSpec as P

HEADS = 16
KV_HEADS = 4
HDIM = 128
BUCKET = 128
GROUP = HEADS // KV_HEADS
NEG = -1e30
PACK = 16
COUNT_ROW = 8
MARK_ROW = 9
RANK_ROW = 10

f32 = jnp.float32
bf16 = jnp.bfloat16
NN = (((1,), (0,)), ((), ()))
NT = (((1,), (1,)), ((), ()))
TN = (((0,), (0,)), ((), ()))
VMEM = pl.BlockSpec(memory_space=pltpu.VMEM)
SMEM = pl.BlockSpec(memory_space=pltpu.SMEM)
HBM = pl.BlockSpec(memory_space=pltpu.HBM)
LARGE = pltpu.CompilerParams(vmem_limit_bytes=24 * 1024 * 1024)
LOADS = pl.CostEstimate(flops=10**10, transcendentals=0, bytes_accessed=10**7)
SMALL = pltpu.CompilerParams(vmem_limit_bytes=6 * 1024 * 1024)


def in_hbm(*arrays):
    return [pltpu.with_memory_space_constraint(array, pltpu.HBM) for array in arrays]


def moved(array, axis, apart):
    return lax.ppermute(array, axis, [(i, i ^ apart) for i in range(lax.axis_size(axis))])


def rounds(size):
    found, base = [], 2
    while base < size:
        found.append([base + 1] if base * 2 >= size else [base + 1, 2 * base + 1, 3 * base + 1])
        base *= 2 if base * 2 >= size else 4
    return found


def slot_order(size):
    order = [0, 1]
    for offsets in rounds(size):
        order = order + [d ^ near for d in offsets for near in order]
    return order


def iota(shape, dim):
    return lax.broadcasted_iota(jnp.int32, shape, dim)


def token_kernel(out_ref):
    out_ref[...] = iota(out_ref.shape, 1)


def pack_kernel(
    row_ref, count_ref, token_ref, rank_ref, keys_ref, values_ref, kv_ref, out_ref, meta_ref
):
    wide = keys_ref.shape[2]
    kv_ref[:, :wide] = keys_ref[0]
    kv_ref[:, wide:] = values_ref[0]
    length = kv_ref.shape[0]
    row = row_ref[0, 0]
    pick = (token_ref[...] == row).astype(bf16)
    picked = jnp.dot(pick, kv_ref[...], preferred_element_type=f32)
    ranks = rank_ref[...].astype(f32)
    mark = jnp.sum(jnp.where(token_ref[:1] == row, ranks, 0.0), axis=1, keepdims=True)
    mark = (mark >= BUCKET).astype(f32)
    at = iota((PACK, HDIM), 0)
    tile = jnp.zeros((PACK, HDIM), f32)
    for j in range(2 * KV_HEADS):
        tile = jnp.where(at == j, picked[:, j * HDIM : (j + 1) * HDIM], tile)
    tile = jnp.where(at == COUNT_ROW, count_ref[0, 0].astype(f32), tile)
    tile = jnp.where(at == MARK_ROW, mark, tile)
    tile = jnp.where(at == RANK_ROW, ranks, tile)
    out_ref[...] = tile.astype(bf16)
    at = iota((8, length), 0)
    meta = jnp.where(at == 0, row.astype(f32), 0.0)
    meta_ref[...] = meta


def columns(j):
    return slice(j * HDIM, (j + 1) * HDIM)


def stacked(ref, j):
    return jnp.concatenate([ref[0, :, columns(j * GROUP + g)] for g in range(GROUP)], 0)


def by_bucket(rows, first):
    low = jnp.concatenate([first] * GROUP, 0).astype(bf16)
    high = jnp.concatenate([1.0 - first] * GROUP, 0).astype(bf16)
    return jnp.concatenate([rows * low, rows * high], 1)


def score_kernel(
    query_ref, grad_ref, kv_ref, far_ref, packs_ref, sink_ref,
    weight_ref, up_ref, stats_ref, keys2_ref, home_ref, first_ref, same_ref,
):
    same_ref[...] = packs_ref[...]
    length = kv_ref.shape[0]
    span = 2 * length
    group = GROUP * length
    scale = HDIM**-0.5
    tiles = packs_ref[...].astype(f32)
    own_ranks = tiles[RANK_ROW : RANK_ROW + 1]
    far_ranks = tiles[PACK + RANK_ROW : PACK + RANK_ROW + 1]
    ranks = jnp.concatenate([own_ranks, far_ranks], 1)
    move = (iota((span, span), 0).astype(f32) == ranks).astype(f32)
    home_ref[...] = jnp.transpose(move).astype(bf16)
    in_order = jnp.dot(
        move.astype(bf16), jnp.concatenate([kv_ref[...], far_ref[...]], 0), preferred_element_type=f32
    ).astype(bf16)
    column = jnp.transpose(jnp.broadcast_to(own_ranks, (length, length)))
    first = (column < BUCKET).astype(f32)
    first_ref[...] = first
    for j in range(KV_HEADS):
        at = slice(j * group, (j + 1) * group)
        keys = jnp.concatenate([in_order[:BUCKET, columns(j)], in_order[BUCKET:, columns(j)]], 1)
        keys2_ref[:, 2 * j * HDIM : 2 * (j + 1) * HDIM] = keys
        to = columns(KV_HEADS + j)
        values = jnp.concatenate([in_order[:BUCKET, to], in_order[BUCKET:, to]], 1)
        query = by_bucket(stacked(query_ref, j), first)
        grad = by_bucket(stacked(grad_ref, j), first)
        score = lax.dot_general(keys, query, NT, preferred_element_type=f32) * scale
        heads = range(j * GROUP, (j + 1) * GROUP)
        sink = jnp.concatenate([jnp.broadcast_to(sink_ref[:, h : h + 1], (1, length)) for h in heads], 1)
        top = jnp.maximum(jnp.max(score, axis=0, keepdims=True), sink)
        weight = jnp.exp(score - top)
        sink_weight = jnp.exp(sink - top)
        weight_ref[:, at] = weight
        up = lax.dot_general(values, grad, NT, preferred_element_type=f32)
        up_ref[:, at] = up
        stats_ref[0:1, at] = top
        stats_ref[1:2, at] = jnp.sum(weight, axis=0, keepdims=True) + sink_weight
        stats_ref[2:3, at] = jnp.sum(weight * up, axis=0, keepdims=True)
        stats_ref[3:4, at] = sink_weight


def terms_kernel(
    slots, query_ref, grad_ref, weight_ref, up_ref, stats_ref, packs_ref,
    out_hbm, ds_ref, half_ref, slot_keys_ref, out_ref, rows_ref, sinks_ref, tiles_ref, sem,
):
    length = query_ref.shape[1]
    group = GROUP * length
    padded = -(-slots // 16) * 16
    order = slot_order(slots)
    scale = HDIM**-0.5
    tiles_ref[...] = packs_ref[...].astype(f32)

    def chosen(row):
        part = tiles_ref[pl.ds(row, slots, stride=PACK), :]
        if padded > slots:
            part = jnp.concatenate([part, jnp.zeros((padded - slots, HDIM), f32)], 0)
        return part

    slot_keys = [chosen(j).astype(bf16) for j in range(KV_HEADS)]
    slot_values = [chosen(KV_HEADS + j).astype(bf16) for j in range(KV_HEADS)]
    slot_keys_ref[...] = jnp.concatenate(slot_keys, 1)
    own_marks = (tiles_ref[RANK_ROW : RANK_ROW + 1] >= BUCKET).astype(f32)
    slot_at = iota((padded, length), 0)
    bias = jnp.log(jnp.maximum(chosen(COUNT_ROW), 1.0))
    same = (slot_at < 2) & (chosen(MARK_ROW) == own_marks)
    bias = jnp.where(same | (slot_at >= slots), NEG, bias)
    query = [stacked(query_ref, j) for j in range(KV_HEADS)]
    grad = [stacked(grad_ref, j) for j in range(KV_HEADS)]

    def against(parts, rows):
        return jnp.concatenate(
            [lax.dot_general(part, row, NT, preferred_element_type=f32) for part, row in zip(parts, rows)], 1
        )

    score = against(slot_keys, query) * scale + jnp.concatenate([bias] * HEADS, 1)
    up = against(slot_values, grad)
    pair_top = stats_ref[0:1]
    top = jnp.maximum(pair_top, jnp.max(score, axis=0, keepdims=True))
    weight = jnp.exp(score - top)
    pair_scale = jnp.exp(pair_top - top)
    inverse = 1.0 / (pair_scale * stats_ref[1:2] + jnp.sum(weight, axis=0, keepdims=True))
    pair_scale = pair_scale * inverse
    prob = weight * inverse
    delta = pair_scale * stats_ref[2:3] + jnp.sum(prob * up, axis=0, keepdims=True)
    ds = (prob * (up - delta)).astype(bf16)
    half = prob.astype(bf16)
    ds_ref[length:] = ds
    rows_ref[0:1] = pair_scale
    rows_ref[1:2] = delta
    sink_rows = pair_scale * stats_ref[3:4] * delta
    for h in range(HEADS):
        sinks_ref[h : h + 1] = sink_rows[:, h * length : (h + 1) * length]
    sinks = jnp.sum(sinks_ref[...], axis=1, keepdims=True)
    sinks = jnp.where(iota((HEADS, HDIM), 0) == iota((HEADS, HDIM), 1), -sinks, 0.0)
    sinks = jnp.sum(sinks, axis=0, keepdims=True)
    high = sinks.astype(bf16).astype(f32)
    ends = (high, sinks - high)

    def piece(first, second):
        shape = out_ref.shape[1:]
        upper = jnp.broadcast_to(jnp.concatenate([first, ends[0]], 1), shape)
        lower = jnp.broadcast_to(jnp.concatenate([second, ends[1]], 1), shape)
        return jnp.where(iota(shape, 0) == 0, upper, lower).astype(bf16)

    nothing = jnp.zeros((1, KV_HEADS * HDIM), f32)
    out_ref[...] = jnp.broadcast_to(piece(nothing, nothing)[None], out_ref.shape)
    key_rows, value_rows = (
        jnp.concatenate(
            [
                lax.dot_general(left[:, j * group : (j + 1) * group], right[j], NN, preferred_element_type=f32)
                for j in range(KV_HEADS)
            ],
            1,
        )
        for left, right in ((ds, query), (half, grad))
    )
    key_rows = key_rows * scale
    first = lax.axis_index("dp") * slots
    for slot in range(slots):
        out_ref[first + (lax.axis_index("ctx") ^ order[slot])] = piece(
            key_rows[slot : slot + 1], value_rows[slot : slot + 1]
        )
    copy = pltpu.make_async_copy(out_ref, out_hbm, sem)
    copy.start()

    @pl.loop(0, KV_HEADS)
    def _(j):
        at = pl.ds(pl.multiple_of(j * group, group), group)
        pair_prob = weight_ref[:, at] * rows_ref[0:1, at]
        ds_ref[pl.ds(0, length), at] = (pair_prob * (up_ref[:, at] - rows_ref[1:2, at])).astype(bf16)
        half_ref[:, at] = pair_prob.astype(bf16)

    copy.wait()


def gradient_kernel(
    query_ref, grad_ref, ds_ref, half_ref, slot_keys_ref, keys2_ref, home_ref, first_ref,
    dq_hbm, own_grad_ref, *refs,
):
    far_grad_refs, (dq_ref, sems) = refs[:-2], refs[-2:]
    length = first_ref.shape[0]
    group = GROUP * length
    wide = KV_HEADS * HDIM
    scale = HDIM**-0.5
    mine = jnp.concatenate([first_ref[...]] * GROUP, 0) > 0.5
    sent = []
    grads = [[], []]
    for j in range(KV_HEADS):
        at = slice(j * group, (j + 1) * group)
        slot_keys = slot_keys_ref[:, columns(j)]
        keys = jnp.concatenate(
            [keys2_ref[:, 2 * j * HDIM : 2 * (j + 1) * HDIM], jnp.concatenate([slot_keys, slot_keys], 1)], 0
        )
        dq = lax.dot_general(ds_ref[:, at], keys, TN, preferred_element_type=f32)
        dq = (jnp.where(mine, dq[:, :HDIM], dq[:, HDIM:]) * scale).astype(bf16)
        for g in range(GROUP):
            dq_ref[:, columns(j * GROUP + g)] = dq[g * length : (g + 1) * length]
        to = pl.ds(j * GROUP * HDIM, GROUP * HDIM)
        copy = pltpu.make_async_copy(dq_ref.at[:, to], dq_hbm.at[0, :, to], sems.at[j])
        copy.start()
        sent.append(copy)
        query = by_bucket(stacked(query_ref, j), first_ref[...])
        grad = by_bucket(stacked(grad_ref, j), first_ref[...])
        dk = lax.dot_general(ds_ref[:length, at], query, NN, preferred_element_type=f32) * scale
        dv = lax.dot_general(half_ref[:, at], grad, NN, preferred_element_type=f32)
        for i, part in enumerate((dk, dv)):
            grads[i].append(jnp.concatenate([part[:, :HDIM], part[:, HDIM:]], 0))
    for i in range(2):
        in_order = jnp.concatenate(grads[i], 1)
        high = in_order.astype(bf16)
        low = (in_order - high.astype(f32)).astype(bf16)
        back = jnp.dot(home_ref[...], high, preferred_element_type=f32)
        rest = jnp.dot(home_ref[:length], low, preferred_element_type=f32)
        own_grad_ref[:, i * wide : (i + 1) * wide] = back[:length] + rest
        far_grad_refs[i][...] = back[length:].astype(bf16)
    for copy in sent:
        copy.wait()


def total_kernel(meta_ref, own_ref, key_recv_ref, value_recv_ref, total_ref, row_ref):
    length = own_ref.shape[0]
    mine = iota((length, HDIM), 0).astype(f32) == meta_ref[0:1]
    for i, recv_ref in enumerate((key_recv_ref, value_recv_ref)):
        for j in range(KV_HEADS):
            at = columns(i * KV_HEADS + j)
            total = own_ref[:, at] + recv_ref[:, columns(j)].astype(f32)
            total_ref[:, at] = total.astype(bf16)
            row = jnp.sum(jnp.where(mine, total, 0.0), axis=0, keepdims=True)
            row_ref[i : i + 1, columns(j)] = row


def last_kernel(slots, meta_ref, total_ref, row_ref, terms_ref, dk_ref, dv_ref, sink_ref):
    length = total_ref.shape[0]
    wide = KV_HEADS * HDIM
    ends = jnp.sum(terms_ref[:, :, wide:].astype(f32), axis=0)
    sink_ref[...] = (ends[0:1] + ends[1:2])[:, :HEADS]
    first = lax.axis_index("dp") * slots
    row = row_ref[0:2] + jnp.sum(terms_ref[pl.ds(first, slots), :, :wide].astype(f32), axis=0)
    mine = iota((length, HDIM), 0).astype(f32) == meta_ref[0:1]
    for i, out_ref in enumerate((dk_ref, dv_ref)):
        for j in range(KV_HEADS):
            total = total_ref[:, columns(i * KV_HEADS + j)].astype(f32)
            out_ref[0, :, columns(j)] = jnp.where(mine, row[i : i + 1, columns(j)], total).astype(bf16)


def on_device(
    query_rows, key_rows, value_rows, grad_rows, bucket_rank, sample_rows, sample_count, sink_logit
):
    length = query_rows.shape[1]
    wide = KV_HEADS * HDIM
    slots = lax.axis_size("ctx")
    rows = HEADS * HDIM
    token = pl.pallas_call(
        token_kernel,
        out_shape=jax.ShapeDtypeStruct((PACK, length), jnp.int32),
        out_specs=VMEM,
        compiler_params=SMALL,
        cost_estimate=LOADS,
        name="token_lanes",
    )()
    sample_rows, sample_count, token = lax.optimization_barrier((sample_rows, sample_count, token))
    kv, tile, meta = pl.pallas_call(
        pack_kernel,
        out_shape=[
            jax.ShapeDtypeStruct((length, 2 * wide), bf16),
            jax.ShapeDtypeStruct((PACK, HDIM), bf16),
            jax.ShapeDtypeStruct((8, length), f32),
        ],
        in_specs=[SMEM] * 2 + [VMEM] * 4,
        out_specs=[VMEM] * 3,
        compiler_params=SMALL,
        cost_estimate=LOADS,
        name="pack_sample",
    )(sample_rows, sample_count, token, bucket_rank, key_rows, value_rows)

    far_tile = moved(tile, "ctx", 1)
    kv, far_tile = lax.optimization_barrier((kv, far_tile))
    far_kv = moved(kv, "ctx", 1)
    packs = jnp.concatenate([tile, far_tile], 0)
    by_token = jax.ShapeDtypeStruct((length, rows), f32)
    weight, up, stats, keys2, home, first, same = pl.pallas_call(
        score_kernel,
        out_shape=[
            by_token,
            by_token,
            jax.ShapeDtypeStruct((8, rows), f32),
            jax.ShapeDtypeStruct((length, 2 * wide), bf16),
            jax.ShapeDtypeStruct((2 * length, 2 * length), bf16),
            jax.ShapeDtypeStruct((length, length), f32),
            jax.ShapeDtypeStruct(packs.shape, bf16),
        ],
        in_specs=[VMEM] * 6,
        out_specs=[VMEM] * 7,
        compiler_params=LARGE,
        cost_estimate=pl.CostEstimate(
            flops=8 * length * length * rows, transcendentals=2 * length * rows, bytes_accessed=20 * length * rows
        ),
        name="pair_scores",
    )(query_rows, grad_rows, kv, far_kv, packs, sink_logit[None])
    for offsets in rounds(slots):
        arrived = [moved(packs, "ctx", d) for d in offsets]
        packs = jnp.concatenate([same] + arrived, 0)
        same = packs
    devices = slots * lax.axis_size("dp")
    padded = -(-slots // 16) * 16
    terms, ds, half, slot_keys = pl.pallas_call(
        functools.partial(terms_kernel, slots),
        out_shape=[
            jax.ShapeDtypeStruct((devices, 2, wide + HDIM), bf16),
            jax.ShapeDtypeStruct((length + padded, rows), bf16),
            jax.ShapeDtypeStruct((length, rows), bf16),
            jax.ShapeDtypeStruct((padded, wide), bf16),
        ],
        in_specs=[VMEM] * 6,
        out_specs=[HBM] + [VMEM] * 3,
        scratch_shapes=[
            pltpu.VMEM((devices, 2, wide + HDIM), bf16),
            pltpu.VMEM((8, rows), f32),
            pltpu.VMEM((HEADS, length), f32),
            pltpu.VMEM((slots * PACK, HDIM), f32),
            pltpu.SemaphoreType.DMA,
        ],
        compiler_params=LARGE,
        name="slot_terms",
    )(query_rows, grad_rows, weight, up, stats, packs)
    terms = lax.all_to_all(terms, ("dp", "ctx"), 0, 0, tiled=True)
    dq, own, *far = pl.pallas_call(
        gradient_kernel,
        out_shape=[
            jax.ShapeDtypeStruct((1, length, rows), bf16),
            jax.ShapeDtypeStruct((length, 2 * wide), f32),
        ]
        + [jax.ShapeDtypeStruct((length, 2 * wide // 2), bf16)] * 2,
        in_specs=[VMEM] * 8,
        out_specs=[HBM] + [VMEM] * 3,
        scratch_shapes=[pltpu.VMEM((length, rows), bf16), pltpu.SemaphoreType.DMA((KV_HEADS,))],
        compiler_params=LARGE,
        cost_estimate=pl.CostEstimate(
            flops=12 * length * length * rows, transcendentals=0, bytes_accessed=20 * length * rows
        ),
        name="gradients",
    )(query_rows, grad_rows, ds, half, slot_keys, keys2, home, first)
    recv = [moved(part, "ctx", 1) for part in far]
    total, sampled = pl.pallas_call(
        total_kernel,
        out_shape=[
            jax.ShapeDtypeStruct((length, 2 * wide), bf16),
            jax.ShapeDtypeStruct((8, wide), f32),
        ],
        in_specs=[VMEM] * 4,
        out_specs=[VMEM] * 2,
        compiler_params=SMALL,
        name="pair_total",
    )(meta, own, *recv)
    dk, dv, sink_grad = pl.pallas_call(
        functools.partial(last_kernel, slots),
        out_shape=[jax.ShapeDtypeStruct((1, length, wide), bf16)] * 2
        + [jax.ShapeDtypeStruct((1, HEADS), f32)],
        in_specs=[VMEM] * 4,
        out_specs=[VMEM] * 3,
        compiler_params=SMALL,
        name="add_up",
    )(meta, total, sampled, terms)
    return dq, dk, dv, sink_grad[0]


def solution(mesh):
    return jax.shard_map(
        on_device,
        mesh=mesh,
        in_specs=(
            P("dp", "ctx", None),
            P("dp", "ctx", None),
            P("dp", "ctx", None),
            P("dp", "ctx", None),
            P("dp", "ctx"),
            P("dp", "ctx"),
            P("dp", "ctx"),
            P(),
        ),
        out_specs=(P("dp", "ctx", None), P("dp", "ctx", None), P("dp", "ctx", None), P()),
        check_vma=False,
    )
```

```python
import functools

import jax
import jax.numpy as jnp
from jax import lax
from jax.experimental import pallas as pl
from jax.experimental.pallas import tpu as pltpu
from jax.sharding import PartitionSpec as P

HEADS = 16
KV_HEADS = 4
HDIM = 128
BUCKET = 128
GROUP = HEADS // KV_HEADS
NEG = -1e30
PACK = 16
COUNT_ROW = 8
MARK_ROW = 9
RANK_ROW = 10

f32 = jnp.float32
bf16 = jnp.bfloat16
NN = (((1,), (0,)), ((), ()))
NT = (((1,), (1,)), ((), ()))
TN = (((0,), (0,)), ((), ()))
VMEM = pl.BlockSpec(memory_space=pltpu.VMEM)
SMEM = pl.BlockSpec(memory_space=pltpu.SMEM)
HBM = pl.BlockSpec(memory_space=pltpu.HBM)
LARGE = pltpu.CompilerParams(vmem_limit_bytes=24 * 1024 * 1024)
LOADS = pl.CostEstimate(flops=10**10, transcendentals=0, bytes_accessed=10**7)
SMALL = pltpu.CompilerParams(vmem_limit_bytes=6 * 1024 * 1024)


def in_hbm(*arrays):
    return [pltpu.with_memory_space_constraint(array, pltpu.HBM) for array in arrays]


def moved(array, axis, apart):
    return lax.ppermute(array, axis, [(i, i ^ apart) for i in range(lax.axis_size(axis))])


def rounds(size):
    found, base = [], 2
    while base < size:
        found.append([base + 1] if base * 2 >= size else [base + 1, 2 * base + 1, 3 * base + 1])
        base *= 2 if base * 2 >= size else 4
    return found


def slot_order(size):
    order = [0, 1]
    for offsets in rounds(size):
        order = order + [d ^ near for d in offsets for near in order]
    return order


def iota(shape, dim):
    return lax.broadcasted_iota(jnp.int32, shape, dim)


def token_kernel(out_ref):
    out_ref[...] = iota(out_ref.shape, 1)


def pack_kernel(
    row_ref, count_ref, token_ref, rank_ref, keys_ref, values_ref, kv_ref, out_ref, meta_ref
):
    wide = keys_ref.shape[2]
    kv_ref[:, :wide] = keys_ref[0]
    kv_ref[:, wide:] = values_ref[0]
    length = kv_ref.shape[0]
    row = row_ref[0, 0]
    pick = (token_ref[...] == row).astype(bf16)
    picked = jnp.dot(pick, kv_ref[...], preferred_element_type=f32)
    ranks = rank_ref[...].astype(f32)
    mark = jnp.sum(jnp.where(token_ref[:1] == row, ranks, 0.0), axis=1, keepdims=True)
    mark = (mark >= BUCKET).astype(f32)
    at = iota((PACK, HDIM), 0)
    tile = jnp.zeros((PACK, HDIM), f32)
    for j in range(2 * KV_HEADS):
        tile = jnp.where(at == j, picked[:, j * HDIM : (j + 1) * HDIM], tile)
    tile = jnp.where(at == COUNT_ROW, count_ref[0, 0].astype(f32), tile)
    tile = jnp.where(at == MARK_ROW, mark, tile)
    tile = jnp.where(at == RANK_ROW, ranks, tile)
    out_ref[...] = tile.astype(bf16)
    at = iota((8, length), 0)
    meta = jnp.where(at == 0, row.astype(f32), 0.0)
    meta_ref[...] = meta


def columns(j):
    return slice(j * HDIM, (j + 1) * HDIM)


def stacked(ref, j):
    return jnp.concatenate([ref[0, :, columns(j * GROUP + g)] for g in range(GROUP)], 0)


def by_bucket(rows, first):
    low = jnp.concatenate([first] * GROUP, 0).astype(bf16)
    high = jnp.concatenate([1.0 - first] * GROUP, 0).astype(bf16)
    return jnp.concatenate([rows * low, rows * high], 1)


def score_kernel(
    query_ref, grad_ref, kv_ref, far_ref, packs_ref, sink_ref,
    weight_ref, up_ref, stats_ref, keys2_ref, home_ref, first_ref, same_ref,
):
    same_ref[...] = packs_ref[...]
    length = kv_ref.shape[0]
    span = 2 * length
    group = GROUP * length
    scale = HDIM**-0.5
    tiles = packs_ref[...].astype(f32)
    own_ranks = tiles[RANK_ROW : RANK_ROW + 1]
    far_ranks = tiles[PACK + RANK_ROW : PACK + RANK_ROW + 1]
    ranks = jnp.concatenate([own_ranks, far_ranks], 1)
    move = (iota((span, span), 0).astype(f32) == ranks).astype(f32)
    home_ref[...] = jnp.transpose(move).astype(bf16)
    in_order = jnp.dot(
        move.astype(bf16), jnp.concatenate([kv_ref[...], far_ref[...]], 0), preferred_element_type=f32
    ).astype(bf16)
    column = jnp.transpose(jnp.broadcast_to(own_ranks, (length, length)))
    first = (column < BUCKET).astype(f32)
    first_ref[...] = first
    for j in range(KV_HEADS):
        at = slice(j * group, (j + 1) * group)
        keys = jnp.concatenate([in_order[:BUCKET, columns(j)], in_order[BUCKET:, columns(j)]], 1)
        keys2_ref[:, 2 * j * HDIM : 2 * (j + 1) * HDIM] = keys
        to = columns(KV_HEADS + j)
        values = jnp.concatenate([in_order[:BUCKET, to], in_order[BUCKET:, to]], 1)
        query = by_bucket(stacked(query_ref, j), first)
        grad = by_bucket(stacked(grad_ref, j), first)
        score = lax.dot_general(keys, query, NT, preferred_element_type=f32) * scale
        heads = range(j * GROUP, (j + 1) * GROUP)
        sink = jnp.concatenate([jnp.broadcast_to(sink_ref[:, h : h + 1], (1, length)) for h in heads], 1)
        top = jnp.maximum(jnp.max(score, axis=0, keepdims=True), sink)
        weight = jnp.exp(score - top)
        sink_weight = jnp.exp(sink - top)
        weight_ref[:, at] = weight
        up = lax.dot_general(values, grad, NT, preferred_element_type=f32)
        up_ref[:, at] = up
        stats_ref[0:1, at] = top
        stats_ref[1:2, at] = jnp.sum(weight, axis=0, keepdims=True) + sink_weight
        stats_ref[2:3, at] = jnp.sum(weight * up, axis=0, keepdims=True)
        stats_ref[3:4, at] = sink_weight


def terms_kernel(
    slots, query_ref, grad_ref, weight_ref, up_ref, stats_ref, packs_ref,
    out_hbm, ds_ref, half_ref, slot_keys_ref, out_ref, rows_ref, sinks_ref, tiles_ref, sem,
):
    length = query_ref.shape[1]
    group = GROUP * length
    padded = -(-slots // 16) * 16
    order = slot_order(slots)
    scale = HDIM**-0.5
    tiles_ref[...] = packs_ref[...].astype(f32)

    def chosen(row):
        part = tiles_ref[pl.ds(row, slots, stride=PACK), :]
        if padded > slots:
            part = jnp.concatenate([part, jnp.zeros((padded - slots, HDIM), f32)], 0)
        return part

    slot_keys = [chosen(j).astype(bf16) for j in range(KV_HEADS)]
    slot_values = [chosen(KV_HEADS + j).astype(bf16) for j in range(KV_HEADS)]
    slot_keys_ref[...] = jnp.concatenate(slot_keys, 1)
    own_marks = (tiles_ref[RANK_ROW : RANK_ROW + 1] >= BUCKET).astype(f32)
    slot_at = iota((padded, length), 0)
    bias = jnp.log(jnp.maximum(chosen(COUNT_ROW), 1.0))
    same = (slot_at < 2) & (chosen(MARK_ROW) == own_marks)
    bias = jnp.where(same | (slot_at >= slots), NEG, bias)
    query = [stacked(query_ref, j) for j in range(KV_HEADS)]
    grad = [stacked(grad_ref, j) for j in range(KV_HEADS)]

    def against(parts, rows):
        return jnp.concatenate(
            [lax.dot_general(part, row, NT, preferred_element_type=f32) for part, row in zip(parts, rows)], 1
        )

    score = against(slot_keys, query) * scale + jnp.concatenate([bias] * HEADS, 1)
    up = against(slot_values, grad)
    pair_top = stats_ref[0:1]
    top = jnp.maximum(pair_top, jnp.max(score, axis=0, keepdims=True))
    weight = jnp.exp(score - top)
    pair_scale = jnp.exp(pair_top - top)
    inverse = 1.0 / (pair_scale * stats_ref[1:2] + jnp.sum(weight, axis=0, keepdims=True))
    pair_scale = pair_scale * inverse
    prob = weight * inverse
    delta = pair_scale * stats_ref[2:3] + jnp.sum(prob * up, axis=0, keepdims=True)
    ds = (prob * (up - delta)).astype(bf16)
    half = prob.astype(bf16)
    ds_ref[length:] = ds
    rows_ref[0:1] = pair_scale
    rows_ref[1:2] = delta
    sink_rows = pair_scale * stats_ref[3:4] * delta
    for h in range(HEADS):
        sinks_ref[h : h + 1] = sink_rows[:, h * length : (h + 1) * length]
    sinks = jnp.sum(sinks_ref[...], axis=1, keepdims=True)
    sinks = jnp.where(iota((HEADS, HDIM), 0) == iota((HEADS, HDIM), 1), -sinks, 0.0)
    sinks = jnp.sum(sinks, axis=0, keepdims=True)
    high = sinks.astype(bf16).astype(f32)
    ends = (high, sinks - high)

    def piece(first, second):
        shape = out_ref.shape[1:]
        upper = jnp.broadcast_to(jnp.concatenate([first, ends[0]], 1), shape)
        lower = jnp.broadcast_to(jnp.concatenate([second, ends[1]], 1), shape)
        return jnp.where(iota(shape, 0) == 0, upper, lower).astype(bf16)

    nothing = jnp.zeros((1, KV_HEADS * HDIM), f32)
    out_ref[...] = jnp.broadcast_to(piece(nothing, nothing)[None], out_ref.shape)
    key_rows, value_rows = (
        jnp.concatenate(
            [
                lax.dot_general(left[:, j * group : (j + 1) * group], right[j], NN, preferred_element_type=f32)
                for j in range(KV_HEADS)
            ],
            1,
        )
        for left, right in ((ds, query), (half, grad))
    )
    key_rows = key_rows * scale
    first = lax.axis_index("dp") * slots
    for slot in range(slots):
        out_ref[first + (lax.axis_index("ctx") ^ order[slot])] = piece(
            key_rows[slot : slot + 1], value_rows[slot : slot + 1]
        )
    copy = pltpu.make_async_copy(out_ref, out_hbm, sem)
    copy.start()

    @pl.loop(0, KV_HEADS)
    def _(j):
        at = pl.ds(pl.multiple_of(j * group, group), group)
        pair_prob = weight_ref[:, at] * rows_ref[0:1, at]
        ds_ref[pl.ds(0, length), at] = (pair_prob * (up_ref[:, at] - rows_ref[1:2, at])).astype(bf16)
        half_ref[:, at] = pair_prob.astype(bf16)

    copy.wait()


def gradient_kernel(
    query_ref, grad_ref, ds_ref, half_ref, slot_keys_ref, keys2_ref, home_ref, first_ref,
    dq_hbm, own_grad_ref, *refs,
):
    far_grad_refs, (dq_ref, sems) = refs[:-2], refs[-2:]
    length = first_ref.shape[0]
    group = GROUP * length
    wide = KV_HEADS * HDIM
    scale = HDIM**-0.5
    mine = jnp.concatenate([first_ref[...]] * GROUP, 0) > 0.5
    sent = []
    grads = [[], []]
    for j in range(KV_HEADS):
        at = slice(j * group, (j + 1) * group)
        slot_keys = slot_keys_ref[:, columns(j)]
        keys = jnp.concatenate(
            [keys2_ref[:, 2 * j * HDIM : 2 * (j + 1) * HDIM], jnp.concatenate([slot_keys, slot_keys], 1)], 0
        )
        dq = lax.dot_general(ds_ref[:, at], keys, TN, preferred_element_type=f32)
        dq = (jnp.where(mine, dq[:, :HDIM], dq[:, HDIM:]) * scale).astype(bf16)
        for g in range(GROUP):
            dq_ref[:, columns(j * GROUP + g)] = dq[g * length : (g + 1) * length]
        to = pl.ds(j * GROUP * HDIM, GROUP * HDIM)
        copy = pltpu.make_async_copy(dq_ref.at[:, to], dq_hbm.at[0, :, to], sems.at[j])
        copy.start()
        sent.append(copy)
        query = by_bucket(stacked(query_ref, j), first_ref[...])
        grad = by_bucket(stacked(grad_ref, j), first_ref[...])
        dk = lax.dot_general(ds_ref[:length, at], query, NN, preferred_element_type=f32) * scale
        dv = lax.dot_general(half_ref[:, at], grad, NN, preferred_element_type=f32)
        for i, part in enumerate((dk, dv)):
            grads[i].append(jnp.concatenate([part[:, :HDIM], part[:, HDIM:]], 0))
    for i in range(2):
        in_order = jnp.concatenate(grads[i], 1)
        high = in_order.astype(bf16)
        low = (in_order - high.astype(f32)).astype(bf16)
        back = jnp.dot(home_ref[...], high, preferred_element_type=f32)
        rest = jnp.dot(home_ref[:length], low, preferred_element_type=f32)
        own_grad_ref[:, i * wide : (i + 1) * wide] = back[:length] + rest
        far_grad_refs[i][...] = back[length:].astype(bf16)
    for copy in sent:
        copy.wait()


def total_kernel(meta_ref, own_ref, key_recv_ref, value_recv_ref, dk_ref, dv_ref, block_ref):
    wide = KV_HEADS * HDIM
    row = jnp.max(meta_ref[0:1]).astype(jnp.int32)
    start = pl.multiple_of(row // PACK * PACK, PACK)
    for i, (recv_ref, out_ref) in enumerate(((key_recv_ref, dk_ref), (value_recv_ref, dv_ref))):
        for j in range(KV_HEADS):
            total = own_ref[:, columns(i * KV_HEADS + j)] + recv_ref[:, columns(j)].astype(f32)
            out_ref[0, :, columns(j)] = total.astype(bf16)
        at = slice(i * wide, (i + 1) * wide)
        block_ref[:, at] = own_ref[pl.ds(start, PACK), at] + recv_ref[pl.ds(start, PACK), :].astype(f32)


def last_kernel(
    slots, meta_ref, block_ref, terms_ref, dk_in, dv_in, dk_hbm, dv_hbm, sink_hbm, dk_ref, dv_ref, sink_ref, sems
):
    wide = KV_HEADS * HDIM
    row = jnp.max(meta_ref[0:1]).astype(jnp.int32)
    start = pl.multiple_of(row // PACK * PACK, PACK)
    first = lax.axis_index("dp") * slots
    terms = jnp.sum(terms_ref[pl.ds(first, slots), :, :wide].astype(f32), axis=0)
    mine = iota((PACK, wide), 0) == row - start
    sent = []
    for i, (out_ref, out_hbm) in enumerate(((dk_ref, dk_hbm), (dv_ref, dv_hbm))):
        block = block_ref[:, i * wide : (i + 1) * wide]
        out_ref[...] = (block + jnp.where(mine, terms[i : i + 1], 0.0)).astype(bf16)
        copy = pltpu.make_async_copy(out_ref, out_hbm.at[0, pl.ds(start, PACK), :], sems.at[i])
        copy.start()
        sent.append(copy)
    ends = jnp.sum(terms_ref[:, :, wide:].astype(f32), axis=0)
    sink_ref[...] = (ends[0:1] + ends[1:2])[:, :HEADS]
    copy = pltpu.make_async_copy(sink_ref, sink_hbm, sems.at[2])
    copy.start()
    sent.append(copy)
    for copy in sent:
        copy.wait()


def on_device(
    query_rows, key_rows, value_rows, grad_rows, bucket_rank, sample_rows, sample_count, sink_logit
):
    length = query_rows.shape[1]
    wide = KV_HEADS * HDIM
    slots = lax.axis_size("ctx")
    rows = HEADS * HDIM
    token = pl.pallas_call(
        token_kernel,
        out_shape=jax.ShapeDtypeStruct((PACK, length), jnp.int32),
        out_specs=VMEM,
        compiler_params=SMALL,
        cost_estimate=LOADS,
        name="token_lanes",
    )()
    sample_rows, sample_count, token = lax.optimization_barrier((sample_rows, sample_count, token))
    kv, tile, meta = pl.pallas_call(
        pack_kernel,
        out_shape=[
            jax.ShapeDtypeStruct((length, 2 * wide), bf16),
            jax.ShapeDtypeStruct((PACK, HDIM), bf16),
            jax.ShapeDtypeStruct((8, length), f32),
        ],
        in_specs=[SMEM] * 2 + [VMEM] * 4,
        out_specs=[VMEM] * 3,
        compiler_params=SMALL,
        cost_estimate=LOADS,
        name="pack_sample",
    )(sample_rows, sample_count, token, bucket_rank, key_rows, value_rows)

    far_tile = moved(tile, "ctx", 1)
    kv, far_tile = lax.optimization_barrier((kv, far_tile))
    far_kv = moved(kv, "ctx", 1)
    packs = jnp.concatenate([tile, far_tile], 0)
    by_token = jax.ShapeDtypeStruct((length, rows), f32)
    weight, up, stats, keys2, home, first, same = pl.pallas_call(
        score_kernel,
        out_shape=[
            by_token,
            by_token,
            jax.ShapeDtypeStruct((8, rows), f32),
            jax.ShapeDtypeStruct((length, 2 * wide), bf16),
            jax.ShapeDtypeStruct((2 * length, 2 * length), bf16),
            jax.ShapeDtypeStruct((length, length), f32),
            jax.ShapeDtypeStruct(packs.shape, bf16),
        ],
        in_specs=[VMEM] * 6,
        out_specs=[VMEM] * 7,
        compiler_params=LARGE,
        cost_estimate=pl.CostEstimate(
            flops=8 * length * length * rows, transcendentals=2 * length * rows, bytes_accessed=20 * length * rows
        ),
        name="pair_scores",
    )(query_rows, grad_rows, kv, far_kv, packs, sink_logit[None])
    for offsets in rounds(slots):
        arrived = [moved(packs, "ctx", d) for d in offsets]
        packs = jnp.concatenate([same] + arrived, 0)
        same = packs
    devices = slots * lax.axis_size("dp")
    padded = -(-slots // 16) * 16
    terms, ds, half, slot_keys = pl.pallas_call(
        functools.partial(terms_kernel, slots),
        out_shape=[
            jax.ShapeDtypeStruct((devices, 2, wide + HDIM), bf16),
            jax.ShapeDtypeStruct((length + padded, rows), bf16),
            jax.ShapeDtypeStruct((length, rows), bf16),
            jax.ShapeDtypeStruct((padded, wide), bf16),
        ],
        in_specs=[VMEM] * 6,
        out_specs=[HBM] + [VMEM] * 3,
        scratch_shapes=[
            pltpu.VMEM((devices, 2, wide + HDIM), bf16),
            pltpu.VMEM((8, rows), f32),
            pltpu.VMEM((HEADS, length), f32),
            pltpu.VMEM((slots * PACK, HDIM), f32),
            pltpu.SemaphoreType.DMA,
        ],
        compiler_params=LARGE,
        name="slot_terms",
    )(query_rows, grad_rows, weight, up, stats, packs)
    terms = lax.all_to_all(terms, ("dp", "ctx"), 0, 0, tiled=True)
    dq, own, *far = pl.pallas_call(
        gradient_kernel,
        out_shape=[
            jax.ShapeDtypeStruct((1, length, rows), bf16),
            jax.ShapeDtypeStruct((length, 2 * wide), f32),
        ]
        + [jax.ShapeDtypeStruct((length, 2 * wide // 2), bf16)] * 2,
        in_specs=[VMEM] * 8,
        out_specs=[HBM] + [VMEM] * 3,
        scratch_shapes=[pltpu.VMEM((length, rows), bf16), pltpu.SemaphoreType.DMA((KV_HEADS,))],
        compiler_params=LARGE,
        cost_estimate=pl.CostEstimate(
            flops=12 * length * length * rows, transcendentals=0, bytes_accessed=20 * length * rows
        ),
        name="gradients",
    )(query_rows, grad_rows, ds, half, slot_keys, keys2, home, first)
    recv = [moved(part, "ctx", 1) for part in far]
    grad_shape = jax.ShapeDtypeStruct((1, length, wide), bf16)
    dk, dv, block = pl.pallas_call(
        total_kernel,
        out_shape=[grad_shape, grad_shape, jax.ShapeDtypeStruct((PACK, 2 * wide), f32)],
        in_specs=[VMEM] * 4,
        out_specs=[VMEM] * 3,
        compiler_params=SMALL,
        name="pair_total",
    )(meta, own, *recv)
    dk, dv, sink_grad = pl.pallas_call(
        functools.partial(last_kernel, slots),
        out_shape=[grad_shape, grad_shape, jax.ShapeDtypeStruct((1, HEADS), f32)],
        in_specs=[VMEM] * 3 + [HBM] * 2,
        out_specs=[HBM] * 3,
        scratch_shapes=[pltpu.VMEM((PACK, wide), bf16)] * 2
        + [pltpu.VMEM((1, HEADS), f32), pltpu.SemaphoreType.DMA((3,))],
        input_output_aliases={3: 0, 4: 1},
        compiler_params=SMALL,
        name="add_up",
    )(meta, block, terms, dk, dv)
    return dq, dk, dv, sink_grad[0]


def solution(mesh):
    return jax.shard_map(
        on_device,
        mesh=mesh,
        in_specs=(
            P("dp", "ctx", None),
            P("dp", "ctx", None),
            P("dp", "ctx", None),
            P("dp", "ctx", None),
            P("dp", "ctx"),
            P("dp", "ctx"),
            P("dp", "ctx"),
            P(),
        ),
        out_specs=(P("dp", "ctx", None), P("dp", "ctx", None), P("dp", "ctx", None), P()),
        check_vma=False,
    )
```
